32 devices in a mesh: seq: 4 (over y, core), dp: 8 (over z, x).
Axes of the slice: x: 2, y: 2, z: 4, core: 2. Of those that a mesh axis runs over, the one named last changes fastest.
Arguments:
- tokens: bfloat16 [8, 768, 2048], P('dp', 'seq'), may hold values from -6 to 6
- doc_lengths: int32 [8, 4], P('dp'), may hold values from 1 to 696, as said below
- w_in: bfloat16 [2048, 2048], P(('seq', 'dp')), may hold values from -0.125 to 0.125
- w_forget: bfloat16 [2048, 2048], P(('seq', 'dp')), may hold values from -0.125 to 0.125
- w_gate_out: bfloat16 [2048, 2048], P(('seq', 'dp')), may hold values from -0.125 to 0.125
- w_out: bfloat16 [2048, 2048], P(('seq', 'dp')), may hold values from -0.125 to 0.125
- w_gate: bfloat16 [2048, 5632], P(('seq', 'dp')), may hold values from -0.125 to 0.125
- w_up: bfloat16 [2048, 5632], P(('seq', 'dp')), may hold values from -0.125 to 0.125
- w_down: bfloat16 [2048, 5632], P(('seq', 'dp')), may hold values from -0.078125 to 0.078125
- g_mix: bfloat16 [2048], P(('seq', 'dp')), may hold values from 0.5 to 1.5
- g_out: bfloat16 [2048], P(('seq', 'dp')), may hold values from 0.5 to 1.5
- g_ffn: bfloat16 [2048], P(('seq', 'dp')), may hold values from 0.5 to 1.5
- floor_logit: bfloat16 [2048], P(('seq', 'dp')), may hold values from -2 to 9
- cotangent: bfloat16 [8, 768, 2048], P('dp', 'seq'), may hold values from -6 to 6
Outputs:
- output: bfloat16 [8, 768, 2048], P('dp', 'seq')
- grad_tokens: bfloat16 [8, 768, 2048], P('dp', 'seq')
- grad_w_in: float32 [2048, 2048], P(('seq', 'dp'))
- grad_w_forget: float32 [2048, 2048], P(('seq', 'dp'))
- grad_w_gate_out: float32 [2048, 2048], P(('seq', 'dp'))
- grad_w_out: float32 [2048, 2048], P(('seq', 'dp'))
- grad_w_gate: float32 [2048, 5632], P(('seq', 'dp'))
- grad_w_up: float32 [2048, 5632], P(('seq', 'dp'))
- grad_w_down: float32 [2048, 5632], P(('seq', 'dp'))
- grad_g_mix: float32 [2048], P(('seq', 'dp'))
- grad_g_out: float32 [2048], P(('seq', 'dp'))
- grad_g_ffn: float32 [2048], P(('seq', 'dp'))
- grad_floor_logit: float32 [2048], P(('seq', 'dp'))
The draws below stay inside these ranges and needn't reach their ends.
Inputs may be any that keep to these rules, and one draw needn't show every extreme that they name: `doc_lengths`: in each bucket the 4 lengths sum to at most 768; one document, at a place drawn from the seed, starts in the rows of the bucket's first device and ends in those of its last; rows past the sum are padding.
All inputs are finite; a program needn't handle non-finite values.
Results may differ from the reference program's by a relative error of at most 0.01.
Values may be sent and summed in bfloat16 or wider, within the bound.
No kernel may reach another device: no remote copies, remote signals or barrier semaphores. Data moves between devices by JAX's collectives and lax.ppermute only.
A program may use at most 448 MiB of HBM per device.

```python
import jax
import jax.numpy as jnp
from jax import lax

D = 2048
FF = 5632
TOK_DEV = 192
DOCS = 4
BUCKET = 768
GROUPS = 8
SHORT = 24


def draw_doc_lengths(key, part):
    key = jax.random.fold_in(key, 11)
    key_short, key_pad, key_slot = jax.random.split(key, 3)
    shorts = jax.random.randint(key_short, (GROUPS, DOCS), 1, SHORT + 1)
    padding = jax.random.randint(key_pad, (GROUPS,), 0, TOK_DEV // 2 + 1)
    padding = jnp.where(jnp.arange(GROUPS) == 0, 0, padding)
    slots = jax.random.randint(key_slot, (GROUPS,), 0, DOCS)
    long_len = BUCKET - (DOCS - 1) * SHORT - padding
    picked = jnp.arange(DOCS)[None, :] == slots[:, None]
    return jnp.where(picked, long_len[:, None], shorts).astype(jnp.int32)


def draw_floor_logit(key, part):
    key = jax.random.fold_in(key, 23)
    values = jax.random.uniform(key, (D,), jnp.float32, -2.0, 9.0)
    return values.astype(jnp.bfloat16)


def levels(rng, extent, cuts, smallest, largest):
    level = 1.0
    for dim, shards_of in cuts:
        heights = jax.random.uniform(jax.random.fold_in(jax.random.fold_in(rng, 6), dim), (shards_of,), jnp.float32, smallest / len(cuts), largest / len(cuts))
        level = level * jnp.repeat(jnp.exp(heights), extent[dim] // shards_of).reshape((-1,) + (1,) * (len(extent) - 1 - dim))
    return level


def bell_draw(own_key, extent, width, reach, shards=(), kind=jnp.bfloat16):
    values = width * jax.random.normal(own_key, extent, jnp.float32)
    if shards:
        values = values * levels(own_key, extent, shards, -0.22, 0.18)
    return jnp.clip(values, -reach, reach).astype(kind)


def setup_inputs(seed: int = 0) -> dict:
    splits = jax.random.split(jax.random.key(seed), 15)
    tokens = bell_draw(splits[0], (GROUPS, BUCKET, D), 1.0, 6.0, ((0, 8), (1, 4)))
    doc_lengths = draw_doc_lengths(jax.random.fold_in(splits[14], 71), 0)
    w_in = bell_draw(splits[2], (D, D), D ** -0.5, 0.125, ((0, 32),))
    w_forget = bell_draw(splits[3], (D, D), D ** -0.5, 0.125, ((0, 32),))
    w_gate_out = bell_draw(splits[4], (D, D), D ** -0.5, 0.125, ((0, 32),))
    w_out = bell_draw(splits[5], (D, D), D ** -0.5, 0.125, ((0, 32),))
    w_gate = bell_draw(splits[6], (D, FF), D ** -0.5, 0.125, ((0, 32),))
    w_up = bell_draw(splits[7], (D, FF), D ** -0.5, 0.125, ((0, 32),))
    w_down = bell_draw(splits[8], (D, FF), FF ** -0.5, 0.078125, ((0, 32),))
    g_mix = jnp.clip(1.0 + 0.1 * jax.random.normal(splits[9], (D,), jnp.float32), 0.5, 1.5).astype(jnp.bfloat16)
    g_out = jnp.clip(1.0 + 0.1 * jax.random.normal(splits[10], (D,), jnp.float32), 0.5, 1.5).astype(jnp.bfloat16)
    g_ffn = jnp.clip(1.0 + 0.1 * jax.random.normal(splits[11], (D,), jnp.float32), 0.5, 1.5).astype(jnp.bfloat16)
    floor_logit = draw_floor_logit(jax.random.fold_in(splits[14], 71), 0)
    cotangent = bell_draw(splits[13], (GROUPS, BUCKET, D), 1.0, 6.0, ((0, 8), (1, 4)))
    return dict(tokens=tokens, doc_lengths=doc_lengths, w_in=w_in, w_forget=w_forget, w_gate_out=w_gate_out, w_out=w_out, w_gate=w_gate, w_up=w_up, w_down=w_down, g_mix=g_mix, g_out=g_out, g_ffn=g_ffn, floor_logit=floor_logit, cotangent=cotangent)


EPSILON = 1e-06
HIGHEST_PREC = lax.Precision.HIGHEST

@jax.custom_vjp
def low(v):
    return lax.optimization_barrier(v.astype(jnp.bfloat16)).astype(jnp.float32)

@jax.custom_vjp
def low_back(v):
    return v

def low_keep(v):
    return (low(v), None)

def low_pass(kept, grad):
    return (grad,)

def back_keep(v):
    return (v, None)

def back_low(kept, grad):
    return (low(grad),)
low.defvjp(low_keep, low_pass)
low_back.defvjp(back_keep, back_low)

def linear_combine(first_op, second_op):
    return (first_op[0] * second_op[0], second_op[0] * first_op[1] + second_op[1])

def rms_scaled(values, gains):
    return values * lax.rsqrt(lax.optimization_barrier(jnp.mean(values * values, axis=-1, keepdims=True)) + EPSILON) * gains

def product(left_op, right_op):
    return jnp.dot(left_op, right_op, precision=HIGHEST_PREC, preferred_element_type=jnp.float32)

def product_nt(left_op, right_op):
    return lax.dot_general(left_op, right_op, (((1,), (1,)), ((), ())), precision=HIGHEST_PREC, preferred_element_type=jnp.float32)

def bucket_flags(lengths, row_count):
    doc_ends = jnp.cumsum(lengths).astype(jnp.int32)
    positions = jnp.arange(row_count, dtype=jnp.int32)
    starts_hit = jnp.any(positions[:, None] == doc_ends[None, :-1], axis=1)
    resets = jnp.logical_or(positions == 0, starts_hit)
    live_rows = positions < doc_ends[-1]
    return (resets.astype(jnp.float32)[:, None], live_rows.astype(jnp.float32)[:, None])

def layer(inputs, w_in, w_forget, w_gate_out, w_out, w_gate, w_up, w_down, g_mix, g_out, g_ffn, floor_logit, resets, live_rows):
    mixed_in = low(rms_scaled(inputs, g_mix))
    input_pre = low(low_back(product(mixed_in, w_in)))
    forget_pre = low(low_back(product(mixed_in, w_forget)))
    gate_out_pre = low_back(product(mixed_in, w_gate_out))
    floors = jax.nn.sigmoid(floor_logit)
    forget = (floors + (1.0 - floors) * jax.nn.sigmoid(forget_pre)) * (1.0 - resets)
    drive = jax.nn.silu(input_pre) * live_rows
    _, hidden_states = lax.associative_scan(linear_combine, (forget, (1.0 - forget) * drive), axis=0)
    states = low(low_back(hidden_states))
    branch_in = low(rms_scaled(states, g_out) * jax.nn.silu(gate_out_pre))
    residual = inputs + low_back(product(branch_in, w_out))
    ffn_in = low(rms_scaled(residual, g_ffn))
    gate_pre = low_back(product(ffn_in, w_gate))
    up_pre = low_back(product(ffn_in, w_up))
    middle = low(jax.nn.silu(gate_pre) * up_pre)
    return residual + product_nt(middle, w_down)

def reference(tokens, doc_lengths, w_in, w_forget, w_gate_out, w_out, w_gate, w_up, w_down, g_mix, g_out, g_ffn, floor_logit, cotangent):
    params = tuple((param.astype(jnp.float32) for param in (w_in, w_forget, w_gate_out, w_out, w_gate, w_up, w_down, g_mix, g_out, g_ffn, floor_logit)))

    def one_group(totals, group):
        inputs, lengths, grad_out = group
        resets, live_rows = bucket_flags(lengths, inputs.shape[0])

        def forward(inputs, *weights):
            return layer(inputs, *weights, resets, live_rows)
        outputs, pullback = jax.vjp(forward, inputs, *params)
        grads = pullback(grad_out)
        totals = tuple((running + fresh for running, fresh in zip(totals, grads[1:])))
        return (totals, (outputs.astype(jnp.bfloat16), grads[0].astype(jnp.bfloat16)))
    zeros = tuple((jnp.zeros(param.shape, jnp.float32) for param in params))
    totals, (outputs, grad_tokens) = lax.scan(one_group, zeros, (tokens.astype(jnp.float32), doc_lengths, cotangent.astype(jnp.float32)))
    return (outputs, grad_tokens, totals[0], totals[1], totals[2], totals[3], totals[4], totals[5], totals[6], totals[7], totals[8], totals[9], totals[10])
```

```python
import functools

import jax
import jax.numpy as jnp
from jax import lax
from jax.experimental import pallas as pl
from jax.experimental.pallas import tpu as pltpu
from jax.sharding import Mesh
from jax.sharding import PartitionSpec as P

EPSILON = 1e-06
F32 = jnp.float32
LOW = jnp.bfloat16
TENSOR_PARTS = 8
SWAP = [(0, 1), (1, 0)]
ROWS = 16


def product(left_op, right_op, kind=F32):
    return jnp.dot(left_op, right_op, preferred_element_type=F32).astype(kind)


def product_nt(left_op, right_op, kind=F32):
    return lax.dot_general(
        left_op, right_op, (((1,), (1,)), ((), ())), preferred_element_type=F32
    ).astype(kind)


def product_tn(left_op, right_op, kind=F32):
    return lax.dot_general(
        left_op, right_op, (((0,), (0,)), ((), ())), preferred_element_type=F32
    ).astype(kind)


def norm_forward(values):
    inverse = lax.rsqrt(jnp.mean(values * values, axis=-1, keepdims=True) + EPSILON)
    return (values * inverse, inverse)


def norm_backward(grad_in, normed, inverse, gains):
    grad_gain = jnp.sum(grad_in * normed, axis=0)
    grad_normed = grad_in * gains
    grad_values = inverse * (
        grad_normed - normed * jnp.mean(grad_normed * normed, axis=-1, keepdims=True)
    )
    return (grad_values, grad_gain)


def silu_slope(values):
    sig_values = jax.nn.sigmoid(values)
    return sig_values * (1.0 + values * (1.0 - sig_values))


def row_marks(ends, bucket, first, shape):
    rows = first + lax.broadcasted_iota(jnp.int32, shape, 0)
    docs = ends.shape[1]
    hit = rows == 0
    for doc in range(docs - 1):
        hit = jnp.logical_or(hit, rows == ends[bucket, doc])
    keep = jnp.where(hit, 0.0, 1.0)
    live = jnp.where(rows < ends[bucket, docs - 1], 1.0, 0.0)
    return (keep, live)


def prefix(decay, term, forward):
    rows = lax.broadcasted_iota(jnp.int32, decay.shape, 0)
    for step in (1, 2, 4):
        shift = step if forward else 8 - step
        inside = rows >= step if forward else rows < 8 - step
        moved_term = jnp.where(inside, pltpu.roll(term, shift, 0), 0.0)
        moved_decay = jnp.where(inside, pltpu.roll(decay, shift, 0), 1.0)
        term = term + decay * moved_term
        decay = decay * moved_decay
    return (decay, term)


def forward_kernel(
    buckets,
    segments,
    slots,
    ends,
    pre,
    floors,
    gains,
    forget_out,
    floor_out,
    slope_forget_out,
    slope_input_out,
    states_out,
    scaled_out,
    squares_out,
):
    width = floors.shape[1]
    seg_rows = pre.shape[0] // (buckets * segments)
    floor = floors[...]
    gain = gains[...]
    first_row = lax.broadcasted_iota(jnp.int32, (8, width), 0) == 0

    def one(bucket, segment, block, carry):
        base = pl.multiple_of(slots[bucket * segments + segment] * seg_rows + block * ROWS, ROWS)
        at = pl.ds(base, ROWS)
        keep, live = row_marks(ends, bucket, segment * seg_rows + block * ROWS, (ROWS, width))
        input_pre = pre[at, :width].astype(LOW).astype(F32)
        forget_pre = pre[at, width : 2 * width].astype(LOW).astype(F32)
        gate_pre = pre[at, 2 * width :]
        sig_forget = jax.nn.sigmoid(forget_pre)
        forget = (floor + (1.0 - floor) * sig_forget) * keep
        sig_input = jax.nn.sigmoid(input_pre)
        drive = input_pre * sig_input * live
        term = (1.0 - forget) * drive
        hidden, previous = [], []
        for low in range(0, ROWS, 8):
            decay_part, term_part = prefix(forget[low : low + 8], term[low : low + 8], True)
            here = term_part + decay_part * carry
            previous.append(jnp.where(first_row, carry, pltpu.roll(here, 1, 0)))
            hidden.append(here)
            carry = here[7:8]
        hidden = jnp.concatenate(hidden, axis=0)
        previous = jnp.concatenate(previous, axis=0)
        forget_out[at, :] = forget
        floor_term = (previous - drive) * keep * (1.0 - sig_forget)
        floor_out[at, :] = floor_term
        slope_forget_out[at, :] = floor_term * (1.0 - floor) * sig_forget
        slope_input_out[at, :] = (
            (1.0 - forget) * live * (sig_input * (1.0 + input_pre * (1.0 - sig_input)))
        )
        states = hidden.astype(LOW)
        states_out[at, :] = states
        states = states.astype(F32)
        scaled_out[at, :] = (states * gain * (gate_pre * jax.nn.sigmoid(gate_pre))).astype(LOW)
        squares_out[at, :] = jnp.sum(states * states, axis=1, keepdims=True)
        return carry

    def over_segments(segment, carries):
        def over_blocks(block, carries):
            return tuple(one(b, segment, block, carries[b]) for b in range(buckets))

        return lax.fori_loop(0, seg_rows // ROWS, over_blocks, carries)

    lax.fori_loop(
        0, segments, over_segments, tuple(jnp.zeros((1, width), F32) for _ in range(buckets))
    )


def backward_kernel(
    buckets,
    segments,
    slots,
    grad_branch,
    pre,
    states_in,
    factors,
    gains,
    forget_in,
    floor_in,
    slope_forget_in,
    slope_input_in,
    grads_out,
    branch_out,
    sums_out,
):
    width = gains.shape[1]
    seg_rows = pre.shape[0] // (buckets * segments)
    gain = gains[...]
    last_row = lax.broadcasted_iota(jnp.int32, (8, width), 0) == 7

    def one(bucket, segment, block, carry, floor_sum, gain_sum):
        base = pl.multiple_of(slots[bucket * segments + segment] * seg_rows + block * ROWS, ROWS)
        at = pl.ds(base, ROWS)
        grad_in = grad_branch[at, :]
        gate_pre = pre[at, 2 * width :]
        inverse = factors[at, 0:1]
        mean = factors[at, 1:2]
        normed = states_in[at, :].astype(F32) * inverse
        sig_gate = jax.nn.sigmoid(gate_pre)
        silu_gate = gate_pre * sig_gate
        scaled = normed * gain
        branch_out[at, :] = (scaled * silu_gate).astype(LOW)
        grads_out[at, 2 * width :] = (
            grad_in * scaled * (sig_gate * (1.0 + gate_pre * (1.0 - sig_gate)))
        ).astype(LOW)
        grad_scaled = grad_in * silu_gate
        gain_sum = gain_sum + grad_scaled * normed
        grad_hidden = (inverse * (grad_scaled * gain - normed * mean)).astype(LOW).astype(F32)
        forget = forget_in[at, :]
        term = forget * grad_hidden
        later = []
        for low in reversed(range(0, ROWS, 8)):
            decay_part, term_part = prefix(forget[low : low + 8], term[low : low + 8], False)
            here = term_part + decay_part * carry
            later.insert(0, jnp.where(last_row, carry, pltpu.roll(here, 7, 0)))
            carry = here[0:1]
        grad_total = grad_hidden + jnp.concatenate(later, axis=0)
        grads_out[at, :width] = (grad_total * slope_input_in[at, :]).astype(LOW)
        grads_out[at, width : 2 * width] = (grad_total * slope_forget_in[at, :]).astype(LOW)
        floor_sum = floor_sum + grad_total * floor_in[at, :]
        return (carry, floor_sum, gain_sum)

    def over_segments(step, state):
        segment = segments - 1 - step

        def over_blocks(block_step, state):
            block = seg_rows // ROWS - 1 - block_step
            carries, floor_sum, gain_sum = state
            fresh = []
            for b in range(buckets):
                carry, floor_sum, gain_sum = one(
                    b, segment, block, carries[b], floor_sum, gain_sum
                )
                fresh.append(carry)
            return (tuple(fresh), floor_sum, gain_sum)

        return lax.fori_loop(0, seg_rows // ROWS, over_blocks, state)

    zeros = jnp.zeros((ROWS, width), F32)
    carries = tuple(jnp.zeros((1, width), F32) for _ in range(buckets))
    _, floor_sum, gain_sum = lax.fori_loop(0, segments, over_segments, (carries, zeros, zeros))
    sums_out[0:1, :] = jnp.sum(floor_sum, axis=0, keepdims=True)
    sums_out[1:2, :] = jnp.sum(gain_sum, axis=0, keepdims=True)


VMEM_SPEC = pl.BlockSpec(memory_space=pltpu.VMEM)
SMEM_SPEC = pl.BlockSpec(memory_space=pltpu.SMEM)


def recurrence_forward(buckets, segments, slots, ends, pre, floors, gains):
    rows, width = pre.shape[0], floors.shape[1]
    shape = jax.ShapeDtypeStruct
    return pl.pallas_call(
        functools.partial(forward_kernel, buckets, segments),
        out_shape=tuple(shape((rows, width), F32) for _ in range(4))
        + tuple(shape((rows, width), LOW) for _ in range(2))
        + (shape((rows, 1), F32),),
        in_specs=[SMEM_SPEC] * 2 + [VMEM_SPEC] * 3,
        out_specs=tuple([VMEM_SPEC] * 7),
        compiler_params=pltpu.CompilerParams(vmem_limit_bytes=40 * 1024 * 1024),
        cost_estimate=pl.CostEstimate(
            flops=60 * rows * width, bytes_accessed=36 * rows * width, transcendentals=6 * rows * width
        ),
        name="recurrence_forward",
    )(slots, ends, pre, floors, gains)


def recurrence_backward(buckets, segments, slots, *operands):
    rows, width = operands[0].shape
    shape = jax.ShapeDtypeStruct
    return pl.pallas_call(
        functools.partial(backward_kernel, buckets, segments),
        out_shape=(
            shape((rows, 3 * width), LOW),
            shape((rows, width), LOW),
            shape((2, width), F32),
        ),
        in_specs=[SMEM_SPEC] + [VMEM_SPEC] * len(operands),
        out_specs=tuple([VMEM_SPEC] * 3),
        compiler_params=pltpu.CompilerParams(vmem_limit_bytes=40 * 1024 * 1024),
        cost_estimate=pl.CostEstimate(
            flops=60 * rows * width, bytes_accessed=44 * rows * width, transcendentals=2 * rows * width
        ),
        name="recurrence_backward",
    )(slots, *operands)


class Links:
    def __init__(self, sizes):
        self.sizes = sizes
        self.pairs = sizes["y"] == sizes["core"] == sizes["x"] == 2
        self.plane = ("x", "y", "core")
        self.owners = ("y", "core", "x")

    def place(self, axis):
        return lax.axis_index(axis)

    def slots(self):
        sizes = self.sizes
        x, y, core = jnp.meshgrid(
            jnp.arange(sizes["x"]), jnp.arange(sizes["y"]), jnp.arange(sizes["core"]), indexing="ij"
        )
        if self.pairs:
            x, y, core = x ^ self.place("x"), y ^ self.place("y"), core ^ self.place("core")
            slot = (core * 2 + x) * 2 + y
        else:
            slot = (x * sizes["y"] + y) * sizes["core"] + core
        return slot.reshape(-1).astype(jnp.int32)

    def swap(self, axis, value):
        return lax.ppermute(value, axis, SWAP)

    def rows(self, value):
        if not self.pairs:
            return lax.all_gather(value, self.plane, axis=0, tiled=True)
        half = value.shape[0] // 2
        top, end = value[:half], value[half:]
        x_top, y_end = self.swap("x", top), self.swap("y", end)
        x_end, y_top = self.swap("x", end), self.swap("y", top)
        both_top, both_end = self.swap("y", x_top), self.swap("x", y_end)
        own = jnp.concatenate([top, end, y_top, y_end, x_top, x_end, both_top, both_end], axis=0)
        return jnp.concatenate([own, self.swap("core", own)], axis=0)

    def rows_small(self, value):
        if not self.pairs:
            return lax.all_gather(value, self.plane, axis=0, tiled=True)
        for axis in ("y", "x", "core"):
            value = jnp.concatenate([value, self.swap(axis, value)], axis=0)
        return value

    def sum_rows(self, parts):
        if not self.pairs:
            return lax.psum_scatter(parts, self.plane, scatter_dimension=0, tiled=True).astype(F32)
        rows = parts.shape[0] // 8
        half = rows // 2
        kind = parts.dtype
        parts = parts.reshape(2, 4, rows, -1)
        other = self.swap("core", parts[1])
        chip = (parts[0].astype(F32) + other.astype(F32)).astype(kind).reshape(2, 2, rows, -1)
        top_in, end_in = self.swap("x", chip[1, :, :half]), self.swap("y", chip[:, 1, half:])
        top = chip[0, :, :half].astype(F32) + top_in.astype(F32)
        end = chip[:, 0, half:].astype(F32) + end_in.astype(F32)
        top_in, end_in = self.swap("y", top[1].astype(kind)), self.swap("x", end[1].astype(kind))
        return jnp.concatenate([top[0] + top_in.astype(F32), end[0] + end_in.astype(F32)], axis=0)

    def sum_rows_small(self, parts):
        if not self.pairs:
            return lax.psum_scatter(parts, self.plane, scatter_dimension=0, tiled=True)
        for axis in ("core", "x", "y"):
            half = parts.shape[0] // 2
            parts = parts[:half] + self.swap(axis, parts[half:])
        return parts

    def sum_all_small(self, value):
        planes = self.sizes["z"]
        if not (self.pairs and planes & (planes - 1) == 0):
            return lax.psum(value, ("z",) + self.plane)
        for axis in ("core", "x", "y"):
            value = value + self.swap(axis, value)
        step = 1
        while step < planes:
            value = value + lax.ppermute(value, "z", [(i, i ^ step) for i in range(planes)])
            step *= 2
        return value

    def exchange(self, value):
        return lax.all_to_all(value, self.owners, split_axis=0, concat_axis=0, tiled=True)

    def planes(self, value):
        return lax.all_gather(value, "z", axis=0, tiled=True)

    def sum_planes(self, value):
        return lax.psum_scatter(value, "z", scatter_dimension=0, tiled=True)

    def both_x(self, value):
        if self.sizes["x"] == 1:
            return value
        if self.sizes["x"] != 2:
            return lax.all_gather(value, "x", axis=0, tiled=True)
        other = self.swap("x", value)
        return jnp.where(
            self.place("x") == 0,
            jnp.concatenate([value, other], axis=0),
            jnp.concatenate([other, value], axis=0),
        )


def on_device(
    sizes,
    tokens,
    doc_lengths,
    w_in,
    w_forget,
    w_gate_out,
    w_out,
    w_gate,
    w_up,
    w_down,
    g_mix,
    g_out,
    g_ffn,
    floor_logit,
    cotangent,
):
    links = Links(sizes)
    seq, planes, buckets = sizes["y"] * sizes["core"], sizes["z"], sizes["x"]
    parts = seq * buckets
    width = tokens.shape[2]
    block = w_in.shape[0]
    hidden = w_gate.shape[1]
    slab = width // parts
    seq_place = links.place("y") * sizes["core"] + links.place("core")
    x_place, z_place = links.place("x"), links.place("z")
    owner = (seq_place * planes + z_place) * buckets + x_place

    def to_planes(values):
        lead = values.shape[:-1]
        return jnp.swapaxes(values.reshape(lead + (seq, planes, -1)), -3, -2).reshape(
            lead + (width,)
        )

    def from_planes(values):
        lead = values.shape[:-1]
        return jnp.swapaxes(values.reshape(lead + (planes, seq, -1)), -3, -2).reshape(
            lead + (width,)
        )

    def to_channels(weight):
        return (
            weight.reshape(block, seq, planes, buckets, block)
            .transpose(1, 3, 0, 2, 4)
            .reshape(parts, block, slab)
        )

    def from_channels(grads):
        return (
            grads.reshape(seq, buckets, block, planes, block)
            .transpose(2, 0, 3, 1, 4)
            .reshape(block, width)
        )

    def to_hidden(weight):
        return weight.reshape(block, parts, -1).transpose(1, 0, 2)

    def from_hidden(grads):
        return grads.transpose(1, 0, 2).reshape(block, hidden)

    def own_channels(vector):
        return lax.dynamic_index_in_dim(
            lax.dynamic_index_in_dim(
                vector.reshape(-1, seq, planes, buckets, block), seq_place, 1, keepdims=False
            ),
            x_place,
            2,
            keepdims=False,
        ).reshape(-1, slab)

    def put_channels(vector):
        vector = vector.reshape(-1, 1, planes, 1, block)
        zeros = jnp.zeros((vector.shape[0], seq, planes, buckets, block), F32)
        return lax.dynamic_update_slice(zeros, vector, (0, seq_place, 0, x_place, 0)).reshape(
            -1, width
        )

    mixer = jnp.concatenate([to_channels(w) for w in (w_in, w_forget, w_gate_out)], axis=2)
    full_mixer = links.planes(links.exchange(mixer).reshape(parts * block, 3 * slab))
    full_out = links.planes(to_planes(w_out))
    full_gate, full_up, full_down = (
        links.planes(links.exchange(to_hidden(w)).reshape(parts * block, -1))
        for w in (w_gate, w_up, w_down)
    )
    vectors = jnp.stack([g_mix, g_ffn, g_out, floor_logit]).astype(F32)
    vectors = links.sum_all_small(
        lax.dynamic_update_slice(jnp.zeros((4, width), F32), vectors, (0, owner * block))
    )
    gain_mix, gain_ffn = to_planes(vectors[0]), to_planes(vectors[1])
    own_vectors = own_channels(vectors[2:])
    gain_out = own_vectors[0:1]
    floors = jax.nn.sigmoid(own_vectors[1:2])
    slots = links.slots()
    ends = links.both_x(jnp.cumsum(doc_lengths, axis=1).astype(jnp.int32))

    inputs = to_planes(tokens[0]).astype(F32)
    grad_out = to_planes(cotangent[0])
    normed_in, inverse_in = norm_forward(inputs)
    all_mixed = links.rows((normed_in * gain_mix).astype(LOW))
    all_grad_out = links.rows(grad_out)
    pre = product(all_mixed, full_mixer)
    forget, floor_term, slope_forget, slope_input, states, scaled, squares = recurrence_forward(
        buckets, seq, slots, ends, pre, floors, gain_out
    )
    branch = links.sum_rows(product(scaled, full_out, LOW))
    square_sum = links.sum_rows_small(squares.reshape(parts, -1))
    inverse_h = lax.rsqrt(square_sum.reshape(-1, 1) * (1.0 / width) + EPSILON)
    branch = branch * inverse_h
    residual = inputs + branch

    normed_z, inverse_z = norm_forward(residual)
    all_ffn = links.rows((normed_z * gain_ffn).astype(LOW))
    gate_pre = product(all_ffn, full_gate)
    up_pre = product(all_ffn, full_up)
    silu_gate = jax.nn.silu(gate_pre)
    middle = (silu_gate * up_pre).astype(LOW)
    grad_middle = product(all_grad_out, full_down)
    grad_gate_low = (grad_middle * up_pre * silu_slope(gate_pre)).astype(LOW)
    grad_up_low = (grad_middle * silu_gate).astype(LOW)
    grad_ffn_in = links.sum_rows(
        (product_nt(grad_gate_low, full_gate) + product_nt(grad_up_low, full_up)).astype(LOW)
    )
    output = residual + links.sum_rows(product_nt(middle, full_down, LOW))
    grad_gate_w, grad_up_w, grad_down_w = (
        from_hidden(
            links.exchange(links.sum_planes(product_tn(*ops, LOW)).reshape(parts, block, -1))
        ).astype(F32)
        for ops in (
            (all_ffn, grad_gate_low),
            (all_ffn, grad_up_low),
            (all_grad_out, middle),
        )
    )
    grad_z_norm, grad_g_ffn = norm_backward(grad_ffn_in, normed_z, inverse_z, gain_ffn)
    grad_residual = grad_out.astype(F32) + grad_z_norm

    grad_branch_low = grad_residual.astype(LOW)
    mean_h = jnp.sum(grad_branch_low.astype(F32) * branch, axis=-1, keepdims=True) * (1.0 / width)
    factors = links.rows_small(jnp.concatenate([inverse_h, mean_h], axis=1).T[None])
    factors = jnp.swapaxes(factors, 1, 2).reshape(-1, 2)
    all_grad_branch = links.rows(grad_branch_low)
    grad_branch_in = product_nt(all_grad_branch, full_out)
    grads, branch_in, sums = recurrence_backward(
        buckets,
        seq,
        slots,
        grad_branch_in,
        pre,
        states,
        factors,
        gain_out,
        forget,
        floor_term,
        slope_forget,
        slope_input,
    )
    grad_mixed_in = links.sum_rows(product_nt(grads, full_mixer, LOW))
    grad_mixer = links.exchange(
        links.sum_planes(product_tn(all_mixed, grads, LOW)).reshape(parts, block, 3 * slab)
    )
    grad_in_w, grad_forget_w, grad_gate_out_w = (
        from_channels(grad_mixer[:, :, i * slab : (i + 1) * slab]).astype(F32) for i in range(3)
    )
    grad_out_w = from_planes(
        links.sum_planes(product_tn(branch_in, all_grad_branch, LOW))
    ).astype(F32)
    grad_x_norm, grad_g_mix = norm_backward(grad_mixed_in, normed_in, inverse_in, gain_mix)
    grad_tokens = grad_residual + grad_x_norm
    sums = jnp.concatenate([sums[0:1] * floors * (1.0 - floors), sums[1:2]], axis=0)
    vector_grads = jnp.concatenate(
        [from_planes(grad_g_mix)[None], from_planes(grad_g_ffn)[None], put_channels(sums)], axis=0
    )
    vector_grads = lax.dynamic_slice(
        links.sum_all_small(vector_grads), (0, owner * block), (4, block)
    )
    return (
        from_planes(output.astype(LOW))[None],
        from_planes(grad_tokens.astype(LOW))[None],
        grad_in_w,
        grad_forget_w,
        grad_gate_out_w,
        grad_out_w,
        grad_gate_w,
        grad_up_w,
        grad_down_w,
        vector_grads[0],
        vector_grads[3],
        vector_grads[1],
        vector_grads[2],
    )


def solution(mesh):
    seq, dp = mesh.shape["seq"], mesh.shape["dp"]
    core = 2 if seq % 2 == 0 else 1
    x = max(1, TENSOR_PARTS // seq)
    if dp % x:
        x = 1
    sizes = {"y": seq // core, "core": core, "z": dp // x, "x": x}
    split = Mesh(mesh.devices.reshape(tuple(sizes.values())), tuple(sizes))
    rows = P(("z", "x"), ("y", "core"), None)
    lengths = P(("z", "x"), None)
    matrix = P(("y", "core", "z", "x"), None)
    vector = P(("y", "core", "z", "x"))
    return jax.shard_map(
        functools.partial(on_device, sizes),
        mesh=split,
        in_specs=(rows, lengths) + (matrix,) * 7 + (vector,) * 4 + (rows,),
        out_specs=(rows, rows) + (matrix,) * 7 + (vector,) * 4,
        check_vma=False,
    )
```

```python
import functools
import math

import jax
import jax.numpy as jnp
from jax import lax
from jax.experimental import pallas as pl
from jax.experimental.pallas import tpu as pltpu
from jax.sharding import Mesh
from jax.sharding import PartitionSpec as P

EPSILON = 1e-06
F32 = jnp.float32
LOW = jnp.bfloat16
TENSOR_PARTS = 8
SWAP = [(0, 1), (1, 0)]
ROWS = 16
TILE = 512
SLOTS = 2
COST = 1
VMEM_BYTES = 58 * 1024 * 1024
SPARE_BYTES = 12 * 1024 * 1024
VMEM_SPEC = pl.BlockSpec(memory_space=pltpu.VMEM)
SMEM_SPEC = pl.BlockSpec(memory_space=pltpu.SMEM)
ANY_SPEC = pl.BlockSpec(memory_space=pl.ANY)


def product(left_op, right_op):
    return jnp.dot(left_op, right_op, preferred_element_type=F32)


def product_nt(left_op, right_op):
    return lax.dot_general(
        left_op, right_op, (((1,), (1,)), ((), ())), preferred_element_type=F32
    )


def product_tn(left_op, right_op):
    return lax.dot_general(
        left_op, right_op, (((0,), (0,)), ((), ())), preferred_element_type=F32
    )


def call(
    kernel,
    name,
    outs,
    operands,
    scratch=(),
    smem=0,
    any_from=None,
    any_outs=(),
    cost=(0, 0),
    after=(),
):
    any_from = len(operands) if any_from is None else any_from
    if after:
        inner, count, extra = kernel, len(operands), len(after)

        def kernel(*refs):
            inner(*refs[:count], *refs[count + extra :])

        operands = list(operands) + list(after)
        any_from = min(any_from, count)
    held = list(operands[smem:any_from]) + [
        jax.ShapeDtypeStruct(*out) for i, out in enumerate(outs) if i not in any_outs
    ]
    held = sum(math.prod(array.shape) * array.dtype.itemsize for array in held)
    specs = [
        SMEM_SPEC if i < smem else (ANY_SPEC if i >= any_from else VMEM_SPEC)
        for i in range(len(operands))
    ]
    return pl.pallas_call(
        kernel,
        out_shape=tuple(jax.ShapeDtypeStruct(*out) for out in outs),
        in_specs=specs,
        out_specs=tuple(ANY_SPEC if i in any_outs else VMEM_SPEC for i in range(len(outs))),
        scratch_shapes=list(scratch),
        compiler_params=pltpu.CompilerParams(
            vmem_limit_bytes=VMEM_BYTES if scratch else held + SPARE_BYTES
        ),
        cost_estimate=pl.CostEstimate(
            flops=int(cost[0] * COST), bytes_accessed=int(cost[1] * COST), transcendentals=0
        ),
        name=name,
    )(*operands)


def await_copies(view, sem):
    pltpu.make_async_copy(view, view, sem).wait()


def send(source, target, sem):
    pltpu.make_async_copy(source, target, sem).start()


class Layout:
    def __init__(self, sizes, slot_rows, block, hidden):
        self.seq = sizes["y"] * sizes["core"]
        self.planes = sizes["z"]
        self.buckets = sizes["x"]
        self.parts = self.seq * self.buckets
        self.slot_rows = slot_rows
        self.block = block
        share = hidden // self.parts
        self.split = -(-share // 256) * 128
        self.rest = share - self.split
        self.pieces = sizes["y"] == sizes["core"] == sizes["x"] == 2
        self.strip = self.buckets * block
        half = slot_rows // 2
        self.row_pieces = (
            [(c + s, r) for c in (0, 4) for s, r in ((0, 0), (1, 0), (2, 0), (3, 0), (3, half))]
            if self.pieces
            else [(0, 0)]
        )
        self.row_count = len(self.row_pieces)
        self.plane_count = self.planes if self.pieces else 1
        self.step_rows = SLOTS * slot_rows
        self.steps = self.parts // SLOTS

    def step(self, index):
        return pl.ds(pl.multiple_of(index * self.step_rows, self.step_rows), self.step_rows)

    def await_step(self, target, sems, index):
        for i in range(SLOTS):
            slot = index * SLOTS + i
            first = pl.multiple_of(slot * self.slot_rows, self.slot_rows)
            await_copies(target.at[pl.ds(first, self.slot_rows)], sems.at[slot])

    def fill_rows(self, pieces, target, sems):
        if not self.pieces:
            for slot in range(self.parts):
                at = pl.ds(slot * self.slot_rows, self.slot_rows)
                send(pieces[0].at[at], target.at[at], sems.at[slot])
            return
        for piece, (slot, first) in zip(pieces, self.row_pieces):
            at = pl.ds(slot * self.slot_rows + first, piece.shape[0])
            send(piece, target.at[at], sems.at[slot])

    def fill_weights(self, place, pieces, target, sem, columns=None):
        columns = target.shape[1] if columns is None else columns
        lanes = pl.ds(0, columns)
        if not self.pieces:
            send(pieces[0].at[:, lanes], target, sem)
            return
        if len(pieces) == 1:
            for plane in range(self.planes):
                for s in range(self.seq):
                    send(
                        pieces[0].at[pl.ds((plane * self.seq + s) * self.strip, self.strip), lanes],
                        target.at[pl.ds((s * self.planes + plane) * self.strip, self.strip)],
                        sem,
                    )
            return
        for step, piece in enumerate(pieces):
            plane = lax.rem(place - step + self.planes, self.planes)
            for s in range(self.seq):
                first = pl.multiple_of((s * self.planes + plane) * self.strip, self.strip)
                send(
                    piece.at[pl.ds(s * self.strip, self.strip), lanes],
                    target.at[pl.ds(first, self.strip)],
                    sem,
                )

    def fill_channels(self, place, pieces, target, sem):
        if len(pieces) == 1:
            send(pieces[0], target, sem)
            return
        for step, piece in enumerate(pieces):
            plane = lax.rem(place - step + self.planes, self.planes)
            first = pl.multiple_of(plane * self.block, self.block)
            send(piece, target.at[pl.ds(first, self.block)], sem)

    def strip_row(self, index):
        if not self.pieces:
            return index * self.strip
        return pl.multiple_of(
            ((index % self.planes) * self.seq + index // self.planes) * self.strip, self.strip
        )

    def weight_grads(self, out, staged, sem, step, value):
        if not self.pieces:
            rows = pl.ds(pl.multiple_of(step * TILE, TILE), TILE)
            staged[rows, :] = value
            send(staged.at[rows], out.at[rows], sem)
            return
        per = TILE // self.strip
        for i in range(per):
            rows = pl.ds(self.strip_row(step * per + i), self.strip)
            staged[rows, :] = value[i * self.strip : (i + 1) * self.strip]
            send(staged.at[rows], out.at[rows], sem)


def to_channels_kernel(layout, *refs):
    *weights, out = refs
    block, width = layout.block, layout.block * layout.planes
    for i, weight in enumerate(weights):
        for s in range(layout.seq):
            for z in range(layout.planes):
                for x in range(layout.buckets):
                    first = ((s * layout.planes + z) * layout.buckets + x) * block
                    to = i * width + z * block
                    out[s * layout.buckets + x, :, to : to + block] = weight[
                        :, first : first + block
                    ]


def from_channels_kernel(layout, grads, gains, *refs):
    count = (len(refs) - 1) // 2
    weights, outs, gain_out = refs[:count], refs[count:-1], refs[-1]
    block, width = layout.block, layout.block * layout.planes
    total = jnp.zeros((block, 1), F32)
    for i, (weight, out) in enumerate(zip(weights, outs)):
        for s in range(layout.seq):
            for z in range(layout.planes):
                for x in range(layout.buckets):
                    first = ((s * layout.planes + z) * layout.buckets + x) * block
                    at = i * width + z * block
                    out[:, first : first + block] = grads[
                        s * layout.buckets + x, :, at : at + block
                    ].astype(F32)
        total = total + jnp.sum(out[...] * weight[...].astype(F32), axis=1, keepdims=True)
    gain_out[...] = total / gains[...]


def to_hidden_kernel(layout, first, size, *refs):
    *weights, out = refs
    share = weights[0].shape[1] // layout.parts
    for i, weight in enumerate(weights):
        for part in range(layout.parts):
            at = part * share + first
            out[part, :, i * size : (i + 1) * size] = weight[:, at : at + size]
    used = len(weights) * size
    if used < out.shape[2]:
        out[:, :, used:] = jnp.zeros((layout.parts, layout.block, out.shape[2] - used), LOW)


def from_hidden_kernel(layout, first, second, gains, *refs):
    *weights, gate_out, up_out, down_out, gain_out = refs
    split, rest = layout.split, layout.rest
    share = split + rest
    total = jnp.zeros((layout.block, 1), F32)
    for i, out in enumerate((gate_out, up_out, down_out)):
        for part in range(layout.parts):
            at = part * share
            out[:, at : at + split] = first[part, :, i * split : (i + 1) * split].astype(F32)
            out[:, at + split : at + share] = second[part, :, i * rest : (i + 1) * rest].astype(F32)
        if i < len(weights):
            total = total + jnp.sum(out[...] * weights[i][...].astype(F32), axis=1, keepdims=True)
    gain_out[...] = total / gains[...]


def channel_gain_kernel(grads, weight, gains, floors, out, gain_out, floor_out):
    width = weight.shape[1]
    out[...] = grads[:, :width].astype(F32)
    total = jnp.sum(out[...] * weight[...].astype(F32), axis=1, keepdims=True)
    gain_out[...] = total / gains[...]
    floor = jax.nn.sigmoid(floors[...])
    floor_out[...] = grads[:, width : width + 1].astype(F32) * floor * (1.0 - floor)


def hold_kernel(value, out):
    out[...] = value[...]


def hold(value, after):
    return call(hold_kernel, "hold", [(value.shape, value.dtype)], [value], after=after)[0]


def halves_kernel(by_x, by_y, top, end):
    half = top.shape[0]
    top[...] = by_x[:half, :]
    end[...] = by_y[half:, :]


def row_marks(ends, bucket, first, shape):
    rows = first + lax.broadcasted_iota(jnp.int32, shape, 0)
    docs = ends.shape[1]
    hit = rows == 0
    for doc in range(docs - 1):
        hit = jnp.logical_or(hit, rows == ends[bucket, doc])
    keep = jnp.where(hit, 0.0, 1.0)
    live = jnp.where(rows < ends[bucket, docs - 1], 1.0, 0.0)
    return (keep, live)


def prefix(decay, term, forward):
    rows = lax.broadcasted_iota(jnp.int32, decay.shape, 0)
    for step in (1, 2, 4):
        shift = step if forward else 8 - step
        inside = rows >= step if forward else rows < 8 - step
        moved_term = jnp.where(inside, pltpu.roll(term, shift, 0), 0.0)
        moved_decay = jnp.where(inside, pltpu.roll(decay, shift, 0), 1.0)
        term = term + decay * moved_term
        decay = decay * moved_decay
    return (decay, term)


def mixer_forward_kernel(
    layout,
    slots,
    ends,
    place,
    floors,
    gains,
    *refs,
):
    rows_in = refs[: layout.row_count]
    weights_in = refs[layout.row_count : layout.row_count + layout.plane_count]
    outs, refs = refs[layout.row_count + layout.plane_count :][:7], refs[-14:]
    squares_out, rows_ref, weights, pre = refs[:4]
    row_sems, weight_sem, out_sems = refs[4:7]
    kept = refs[7:]
    (
        forget_out,
        floor_out,
        slope_forget_out,
        slope_input_out,
        gate_out,
        states_out,
        scaled_out,
    ) = kept
    width = floors.shape[1]
    seg_rows = layout.slot_rows
    buckets, segments = layout.buckets, layout.seq
    layout.fill_weights(place[0], weights_in, weights, weight_sem)
    layout.fill_rows(rows_in, rows_ref, row_sems)
    await_copies(weights, weight_sem)

    def multiply(step, _):
        at = layout.step(step)
        layout.await_step(rows_ref, row_sems, step)
        pre[at, :] = product(rows_ref[at, :], weights[...])
        return 0

    lax.fori_loop(0, layout.steps, multiply, 0)
    floor = floors[...]
    gain = gains[...]
    first_row = lax.broadcasted_iota(jnp.int32, (8, width), 0) == 0

    def one(bucket, segment, block, carry):
        base = pl.multiple_of(slots[bucket * segments + segment] * seg_rows + block * ROWS, ROWS)
        at = pl.ds(base, ROWS)
        keep, live = row_marks(ends, bucket, segment * seg_rows + block * ROWS, (ROWS, width))
        input_pre = pre[at, :width].astype(LOW).astype(F32)
        forget_pre = pre[at, width : 2 * width].astype(LOW).astype(F32)
        gate_pre = pre[at, 2 * width :]
        gate_out[at, :] = gate_pre
        sig_forget = jax.nn.sigmoid(forget_pre)
        forget = (floor + (1.0 - floor) * sig_forget) * keep
        sig_input = jax.nn.sigmoid(input_pre)
        drive = input_pre * sig_input * live
        term = (1.0 - forget) * drive
        hidden, previous = [], []
        for low in range(0, ROWS, 8):
            decay_part, term_part = prefix(forget[low : low + 8], term[low : low + 8], True)
            here = term_part + decay_part * carry
            previous.append(jnp.where(first_row, carry, pltpu.roll(here, 1, 0)))
            hidden.append(here)
            carry = here[7:8]
        hidden = jnp.concatenate(hidden, axis=0)
        previous = jnp.concatenate(previous, axis=0)
        forget_out[at, :] = forget
        floor_term = (previous - drive) * keep * (1.0 - sig_forget)
        floor_out[at, :] = floor_term
        slope_forget_out[at, :] = floor_term * (1.0 - floor) * sig_forget
        slope_input_out[at, :] = (
            (1.0 - forget) * live * (sig_input * (1.0 + input_pre * (1.0 - sig_input)))
        )
        states = hidden.astype(LOW)
        states_out[at, :] = states
        scaled_out[at, :] = (
            states.astype(F32) * gain * (gate_pre * jax.nn.sigmoid(gate_pre))
        ).astype(LOW)
        return carry

    def over_segments(segment, carries):
        def over_blocks(block, carries):
            return tuple(one(b, segment, block, carries[b]) for b in range(buckets))

        carries = lax.fori_loop(0, seg_rows // ROWS, over_blocks, carries)
        for b in range(buckets):
            first = pl.multiple_of(slots[b * segments + segment] * seg_rows, seg_rows)
            at = pl.ds(first, seg_rows)
            for i, (ref, out) in enumerate(zip(kept, outs)):
                send(ref.at[at], out.at[at], out_sems.at[i])
        return carries

    lax.fori_loop(
        0, segments, over_segments, tuple(jnp.zeros((1, width), F32) for _ in range(buckets))
    )
    ones = jnp.ones((8, width), LOW)
    for part in range(layout.parts):
        first = pl.multiple_of(slots[part] * seg_rows, seg_rows)
        states = states_out[pl.ds(first, seg_rows), :].astype(F32)
        squares = states * states
        high = squares.astype(LOW)
        rest = (squares - high.astype(F32)).astype(LOW)
        squares_out[part : part + 1, :] = (product_nt(ones, high) + product_nt(ones, rest))[0:1]
    for i, ref in enumerate(kept):
        await_copies(ref, out_sems.at[i])


def mixer_forward(layout, slots, ends, place, floors, gains, rows, weights, after):
    count = layout.parts * layout.slot_rows
    width = floors.shape[1]
    depth = rows[0].shape[1]
    wide = (count, width)
    return call(
        functools.partial(mixer_forward_kernel, layout),
        "mixer_forward",
        [(wide, F32)] * 5 + [(wide, LOW)] * 2 + [((layout.parts, layout.slot_rows), F32)],
        [slots, ends, place, floors, gains, *rows, *weights],
        [
            pltpu.VMEM((count, depth), LOW),
            pltpu.VMEM((depth, 3 * width), LOW),
            pltpu.VMEM((count, 3 * width), F32),
            pltpu.SemaphoreType.DMA((layout.parts,)),
            pltpu.SemaphoreType.DMA,
            pltpu.SemaphoreType.DMA((7,)),
        ]
        + [pltpu.VMEM(wide, F32)] * 5
        + [pltpu.VMEM(wide, LOW)] * 2,
        smem=3,
        any_from=5,
        any_outs=tuple(range(7)),
        after=after,
        cost=(6 * count * width * depth, 2 * count * depth + 6 * depth * width + 24 * count * width),
    )


def branch_kernel(layout, place, scaled, *refs):
    weights_in = refs[:1]
    outs = refs[1:-4]
    weights, staged, sem, out_sem = refs[-4:]
    layout.fill_channels(place[0], weights_in, weights, sem)
    await_copies(weights, sem)
    write_parts(
        layout, outs, staged, out_sem, lambda at: product(scaled[at, :], weights[...])
    )
    await_copies(staged, out_sem)


def write_parts(layout, outs, staged, sem, rows_of):
    per = layout.steps // len(outs)
    for i, out in enumerate(outs):
        start = (len(outs) - 1 - i) * per

        def one(step, _):
            at = layout.step(start + step)
            staged[at, :] = rows_of(at).astype(LOW)
            send(staged.at[at], out.at[layout.step(step)], sem)
            return 0

        lax.fori_loop(0, per, one, 0)


def part_shapes(layout, width):
    count = layout.parts * layout.slot_rows
    if layout.pieces:
        return [((count // 2, width), LOW)] * 2
    return [((count, width), LOW)]


def branch_parts(layout, place, scaled, weights, after):
    count, channels = scaled.shape
    width = weights[0].shape[1]
    return call(
        functools.partial(branch_kernel, layout),
        "branch_parts",
        part_shapes(layout, width),
        [place, scaled, *weights],
        [
            pltpu.VMEM((channels, width), LOW),
            pltpu.VMEM((count, width), LOW),
            pltpu.SemaphoreType.DMA,
            pltpu.SemaphoreType.DMA,
        ],
        smem=1,
        any_from=2,
        any_outs=(0, 1),
        after=after,
        cost=(2 * count * channels * width, 2 * count * width + 2 * channels * width),
    )


def mixer_backward_kernel(
    layout,
    slots,
    place,
    gains,
    *refs,
):
    saved, refs = refs[:6], refs[6:]
    rows_in = refs[: layout.row_count]
    refs = refs[layout.row_count :]
    weights_in, refs = refs[:1], refs[1:]
    mixed_in, refs = refs[: layout.row_count], refs[layout.row_count :]
    (
        grads_out,
        out_grads,
        mixer_grads,
        rows_ref,
        weights,
        mixed,
        grad_branch,
        branch,
        staged_out,
        staged,
        row_sems,
        weight_sem,
        mixed_sems,
        out_sems,
        saved_sems,
        *kept,
    ) = refs
    gate_in, states_in, forget_in, floor_in, slope_forget_in, slope_input_in = kept
    width = gains.shape[1]
    depth = weights.shape[1]
    seg_rows = layout.slot_rows
    buckets, segments = layout.buckets, layout.seq
    layout.fill_channels(place[0], weights_in, weights, weight_sem)
    layout.fill_rows(rows_in, rows_ref, row_sems)
    for i, (source, target) in enumerate(zip(saved, kept)):
        send(source, target, saved_sems.at[i])
    layout.fill_rows(mixed_in, mixed, mixed_sems)
    await_copies(weights, weight_sem)

    def multiply(step, _):
        at = layout.step(step)
        layout.await_step(rows_ref, row_sems, step)
        grad_branch[at, :] = product_nt(rows_ref[at, :depth], weights[...])
        return 0

    lax.fori_loop(0, layout.steps, multiply, 0)
    for i, target in enumerate(kept):
        await_copies(target, saved_sems.at[i])
    gain = gains[...]
    last_row = lax.broadcasted_iota(jnp.int32, (8, width), 0) == 7

    def one(bucket, segment, block, carry, floor_sum):
        base = pl.multiple_of(slots[bucket * segments + segment] * seg_rows + block * ROWS, ROWS)
        at = pl.ds(base, ROWS)
        grad_in = grad_branch[at, :]
        gate_pre = gate_in[at, :]
        factors = rows_ref[at, depth : depth + 4].astype(F32)
        inverse = factors[:, 0:1] + factors[:, 1:2]
        mean = factors[:, 2:3] + factors[:, 3:4]
        normed = states_in[at, :].astype(F32) * inverse
        sig_gate = jax.nn.sigmoid(gate_pre)
        silu_gate = gate_pre * sig_gate
        scaled = normed * gain
        branch[at, :] = (scaled * silu_gate).astype(LOW)
        grads_out[at, 2 * width :] = (
            grad_in * scaled * (sig_gate * (1.0 + gate_pre * (1.0 - sig_gate)))
        ).astype(LOW)
        grad_scaled = grad_in * silu_gate
        grad_hidden = (inverse * (grad_scaled * gain - normed * mean)).astype(LOW).astype(F32)
        forget = forget_in[at, :]
        term = forget * grad_hidden
        later = []
        for low in reversed(range(0, ROWS, 8)):
            decay_part, term_part = prefix(forget[low : low + 8], term[low : low + 8], False)
            here = term_part + decay_part * carry
            later.insert(0, jnp.where(last_row, carry, pltpu.roll(here, 7, 0)))
            carry = here[0:1]
        grad_total = grad_hidden + jnp.concatenate(later, axis=0)
        grads_out[at, :width] = (grad_total * slope_input_in[at, :]).astype(LOW)
        grads_out[at, width : 2 * width] = (grad_total * slope_forget_in[at, :]).astype(LOW)
        floor_sum = floor_sum + grad_total * floor_in[at, :]
        return (carry, floor_sum)

    def over_segments(step, state):
        segment = segments - 1 - step

        def over_blocks(block_step, state):
            block = seg_rows // ROWS - 1 - block_step
            carries, floor_sum = state
            fresh = []
            for b in range(buckets):
                carry, floor_sum = one(b, segment, block, carries[b], floor_sum)
                fresh.append(carry)
            return (tuple(fresh), floor_sum)

        return lax.fori_loop(0, seg_rows // ROWS, over_blocks, state)

    zeros = jnp.zeros((ROWS, width), F32)
    carries = tuple(jnp.zeros((1, width), F32) for _ in range(buckets))
    _, floor_sum = lax.fori_loop(0, segments, over_segments, (carries, zeros))
    staged_out[:, :depth] = product_tn(branch[...], rows_ref[:, :depth]).astype(LOW)
    ones = jnp.ones((ROWS, 128), LOW)
    high = floor_sum.astype(LOW)
    rest = (floor_sum - high.astype(F32)).astype(LOW)
    staged_out[:, depth:] = (product_tn(high, ones) + product_tn(rest, ones)).astype(LOW)
    send(staged_out, out_grads, out_sems.at[0])
    for slot in range(layout.parts):
        at = pl.ds(slot * seg_rows, seg_rows)
        await_copies(mixed.at[at], mixed_sems.at[slot])

    def over_features(step, _):
        columns = pl.ds(pl.multiple_of(step * TILE, TILE), TILE)
        value = product_tn(mixed[:, columns], grads_out[...]).astype(LOW)
        layout.weight_grads(mixer_grads, staged, out_sems.at[1], step, value)
        return 0

    lax.fori_loop(0, mixed.shape[1] // TILE, over_features, 0)
    await_copies(staged_out, out_sems.at[0])
    await_copies(staged, out_sems.at[1])


def mixer_backward(layout, slots, place, gains, saved, rows, weights, mixed, after):
    count = layout.parts * layout.slot_rows
    width = gains.shape[1]
    depth = mixed[0].shape[1]
    wide = depth + 128
    return call(
        functools.partial(mixer_backward_kernel, layout),
        "mixer_backward",
        [
            ((count, 3 * width), LOW),
            ((width, wide), LOW),
            ((depth, 3 * width), LOW),
        ],
        [slots, place, gains, *saved, *rows, *weights, *mixed],
        [
            pltpu.VMEM((count, wide), LOW),
            pltpu.VMEM((width, depth), LOW),
            pltpu.VMEM((count, depth), LOW),
            pltpu.VMEM((count, width), F32),
            pltpu.VMEM((count, width), LOW),
            pltpu.VMEM((width, wide), LOW),
            pltpu.VMEM((depth, 3 * width), LOW),
            pltpu.SemaphoreType.DMA((layout.parts,)),
            pltpu.SemaphoreType.DMA,
            pltpu.SemaphoreType.DMA((layout.parts,)),
            pltpu.SemaphoreType.DMA((2,)),
            pltpu.SemaphoreType.DMA((6,)),
        ]
        + [pltpu.VMEM(array.shape, array.dtype) for array in saved],
        smem=2,
        any_from=3,
        any_outs=(1, 2),
        after=after,
        cost=(10 * count * width * depth, 4 * count * depth + 8 * depth * width + 30 * count * width),
    )


def mixed_grad_kernel(layout, place, grads, *refs):
    weights_in = refs[: layout.plane_count]
    outs = refs[layout.plane_count : -4]
    weights, staged, sem, out_sem = refs[-4:]
    layout.fill_weights(place[0], weights_in, weights, sem)
    await_copies(weights, sem)
    write_parts(
        layout, outs, staged, out_sem, lambda at: product_nt(grads[at, :], weights[...])
    )
    await_copies(staged, out_sem)


def mixed_grad_parts(layout, place, grads, weights, depth, after):
    count, columns = grads.shape
    return call(
        functools.partial(mixed_grad_kernel, layout),
        "mixed_grad_parts",
        part_shapes(layout, depth),
        [place, grads, *weights],
        [
            pltpu.VMEM((depth, columns), LOW),
            pltpu.VMEM((count, depth), LOW),
            pltpu.SemaphoreType.DMA,
            pltpu.SemaphoreType.DMA,
        ],
        smem=1,
        any_from=2,
        any_outs=(0, 1),
        after=after,
        cost=(2 * count * columns * depth, 2 * count * depth + 4 * depth * columns),
    )


def glu_rows(rows_ref, grads_ref, weights, acts, at, width):
    pre = product(rows_ref[at, :], weights[:, : 2 * width])
    gate_pre, up_pre = pre[:, :width], pre[:, width:]
    grad_middle = product(grads_ref[at, :], weights[:, 2 * width : 3 * width])
    sig_gate = jax.nn.sigmoid(gate_pre)
    silu_gate = gate_pre * sig_gate
    acts[at, :width] = (
        grad_middle * up_pre * (sig_gate * (1.0 + gate_pre * (1.0 - sig_gate)))
    ).astype(LOW)
    acts[at, width : 2 * width] = (grad_middle * silu_gate).astype(LOW)
    acts[at, 2 * width : 3 * width] = (silu_gate * up_pre).astype(LOW)
    if 3 * width < acts.shape[1]:
        acts[at, 3 * width :] = jnp.zeros((at.size, acts.shape[1] - 3 * width), LOW)


def glu_grads(layout, rows_ref, grads_ref, acts, out, staged, sem, width):
    def over_features(step, _):
        columns = pl.ds(pl.multiple_of(step * TILE, TILE), TILE)
        left = product_tn(rows_ref[:, columns], acts[:, : 2 * width])
        right = product_tn(grads_ref[:, columns], acts[:, 2 * width :])
        value = jnp.concatenate([left, right], axis=1).astype(LOW)
        layout.weight_grads(out, staged, sem, step, value)
        return 0

    lax.fori_loop(0, rows_ref.shape[1] // TILE, over_features, 0)


def glu_first_kernel(layout, first_count, place, *refs):
    rows_in, refs = refs[: layout.row_count], refs[layout.row_count :]
    grads_in, refs = refs[: layout.row_count], refs[layout.row_count :]
    weights_in, refs = refs[:first_count], refs[first_count:]
    (
        acts_out,
        weight_grads,
        rows_ref,
        grads_ref,
        weights,
        acts,
        staged,
        row_sems,
        grad_sems,
        weight_sem,
        acts_sem,
        out_sem,
    ) = refs
    width = layout.split
    layout.fill_weights(place[0], weights_in, weights, weight_sem)
    layout.fill_rows(rows_in, rows_ref, row_sems)
    layout.fill_rows(grads_in, grads_ref, grad_sems)
    await_copies(weights, weight_sem)

    def one(step, _):
        at = layout.step(step)
        layout.await_step(rows_ref, row_sems, step)
        layout.await_step(grads_ref, grad_sems, step)
        glu_rows(rows_ref, grads_ref, weights, acts, at, width)
        send(acts.at[at], acts_out.at[at], acts_sem)
        return 0

    lax.fori_loop(0, layout.steps, one, 0)
    glu_grads(layout, rows_ref, grads_ref, acts, weight_grads, staged, out_sem, width)
    await_copies(acts, acts_sem)
    await_copies(staged, out_sem)


def glu_first(layout, place, rows, grads, weights):
    count = layout.parts * layout.slot_rows
    depth, columns = rows[0].shape[1], weights[0].shape[1]
    sems = pltpu.SemaphoreType.DMA
    return call(
        functools.partial(glu_first_kernel, layout, len(weights)),
        "glu_first",
        [((count, columns), LOW), ((depth, columns), LOW)],
        [place, *rows, *grads, *weights],
        [
            pltpu.VMEM((count, depth), LOW),
            pltpu.VMEM((count, depth), LOW),
            pltpu.VMEM((depth, columns), LOW),
            pltpu.VMEM((count, columns), LOW),
            pltpu.VMEM((depth, columns), LOW),
            sems((layout.parts,)),
            sems((layout.parts,)),
            sems,
            sems,
            sems,
        ],
        smem=1,
        any_from=1,
        any_outs=(0, 1),
        cost=(4 * count * depth * columns, 4 * count * depth + 4 * depth * columns),
    )


def glu_second_kernel(layout, first_count, place, *refs):
    rows_in, refs = refs[: layout.row_count], refs[layout.row_count :]
    grads_in, refs = refs[: layout.row_count], refs[layout.row_count :]
    first_in, refs = refs[:first_count], refs[first_count:]
    second_in, refs = refs[:first_count], refs[first_count:]
    first_acts_in, acts_out = refs[0], refs[1]
    outs = refs[2:-14]
    (
        rows_ref,
        grads_ref,
        first,
        second,
        first_acts,
        acts,
        row_sems,
        grad_sems,
        first_sem,
        second_sem,
        first_acts_sem,
        acts_sem,
        staged,
        out_sem,
    ) = refs[-14:]
    width = layout.rest
    layout.fill_weights(place[0], second_in, second, second_sem)
    layout.fill_rows(rows_in, rows_ref, row_sems)
    layout.fill_rows(grads_in, grads_ref, grad_sems)
    layout.fill_weights(place[0], first_in, first, first_sem)
    send(first_acts_in.at[:, pl.ds(0, first.shape[1])], first_acts, first_acts_sem)
    await_copies(second, second_sem)

    def one(step, _):
        at = layout.step(step)
        layout.await_step(rows_ref, row_sems, step)
        layout.await_step(grads_ref, grad_sems, step)
        glu_rows(rows_ref, grads_ref, second, acts, at, width)
        send(acts.at[at], acts_out.at[at], acts_sem)
        return 0

    lax.fori_loop(0, layout.steps, one, 0)
    await_copies(first, first_sem)
    await_copies(first_acts, first_acts_sem)
    write_parts(
        layout,
        outs,
        staged,
        out_sem,
        lambda at: product_nt(first_acts[at, :], first[...])
        + product_nt(acts[at, : 2 * width], second[:, : 2 * width]),
    )
    await_copies(acts, acts_sem)
    await_copies(staged, out_sem)


def glu_second(layout, place, rows, grads, first, second, first_acts):
    count = layout.parts * layout.slot_rows
    depth, columns = rows[0].shape[1], second[0].shape[1]
    first_columns = 2 * layout.split
    sems = pltpu.SemaphoreType.DMA
    return call(
        functools.partial(glu_second_kernel, layout, len(first)),
        "glu_second",
        [((count, columns), LOW)] + part_shapes(layout, depth),
        [place, *rows, *grads, *first, *second, first_acts],
        [
            pltpu.VMEM((count, depth), LOW),
            pltpu.VMEM((count, depth), LOW),
            pltpu.VMEM((depth, first_columns), LOW),
            pltpu.VMEM((depth, columns), LOW),
            pltpu.VMEM((count, first_columns), LOW),
            pltpu.VMEM((count, columns), LOW),
            sems((layout.parts,)),
            sems((layout.parts,)),
            sems,
            sems,
            sems,
            sems,
            pltpu.VMEM((count, depth), LOW),
            sems,
        ],
        smem=1,
        any_from=1,
        any_outs=(0, 1, 2),
        cost=(5 * count * depth * columns, 6 * count * depth + 4 * depth * columns),
    )


def glu_third_kernel(layout, place, *refs):
    rows_in, refs = refs[: layout.row_count], refs[layout.row_count :]
    grads_in, refs = refs[: layout.row_count], refs[layout.row_count :]
    acts_in, weight_grads = refs[:2]
    rows_ref, grads_ref, acts, staged, row_sems, grad_sems, acts_sem, out_sem = refs[2:]
    width = layout.rest
    send(acts_in, acts, acts_sem)
    layout.fill_rows(rows_in, rows_ref, row_sems)
    layout.fill_rows(grads_in, grads_ref, grad_sems)
    for slot in range(layout.parts):
        at = pl.ds(slot * layout.slot_rows, layout.slot_rows)
        await_copies(rows_ref.at[at], row_sems.at[slot])
        await_copies(grads_ref.at[at], grad_sems.at[slot])
    await_copies(acts, acts_sem)
    glu_grads(layout, rows_ref, grads_ref, acts, weight_grads, staged, out_sem, width)
    await_copies(staged, out_sem)


def glu_third(layout, place, rows, grads, acts, after):
    count, columns = acts.shape
    depth = rows[0].shape[1]
    sems = pltpu.SemaphoreType.DMA
    return call(
        functools.partial(glu_third_kernel, layout),
        "glu_third",
        [((depth, columns), LOW)],
        [place, *rows, *grads, acts],
        [
            pltpu.VMEM((count, depth), LOW),
            pltpu.VMEM((count, depth), LOW),
            pltpu.VMEM((count, columns), LOW),
            pltpu.VMEM((depth, columns), LOW),
            sems((layout.parts,)),
            sems((layout.parts,)),
            sems,
            sems,
        ],
        smem=1,
        any_from=1,
        any_outs=(0,),
        after=after,
        cost=(2 * count * depth * columns, 4 * count * depth + 2 * depth * columns),
    )[0]


def output_kernel(layout, first_count, place, *refs):
    first_in, refs = refs[:first_count], refs[first_count:]
    second_in, refs = refs[:first_count], refs[first_count:]
    first_acts_in, second_acts_in = refs[:2]
    outs = refs[2:-6]
    first, second, first_acts, second_acts, staged, sems = refs[-6:]
    for weights_in, weights, acts_in, acts, width, i in (
        (first_in, first, first_acts_in, first_acts, layout.split, 0),
        (second_in, second, second_acts_in, second_acts, layout.rest, 2),
    ):
        lanes = pl.ds(2 * width, weights.shape[1])
        layout.fill_weights(
            place[0], [piece.at[:, lanes] for piece in weights_in], weights, sems.at[i]
        )
        send(acts_in.at[:, lanes], acts, sems.at[i + 1])
    await_copies(first, sems.at[0])
    await_copies(first_acts, sems.at[1])
    await_copies(second, sems.at[2])
    await_copies(second_acts, sems.at[3])
    write_parts(
        layout,
        outs,
        staged,
        sems.at[4],
        lambda at: product_nt(first_acts[at, :], first[...])
        + product_nt(second_acts[at, :], second[...]),
    )
    await_copies(staged, sems.at[4])


def output_parts(layout, place, first, second, first_acts, second_acts, depth, after):
    count = first_acts.shape[0]
    widths = first_acts.shape[1] - 2 * layout.split, second_acts.shape[1] - 2 * layout.rest
    return call(
        functools.partial(output_kernel, layout, len(first)),
        "output_parts",
        part_shapes(layout, depth),
        [place, *first, *second, first_acts, second_acts],
        [pltpu.VMEM((depth, width), LOW) for width in widths]
        + [pltpu.VMEM((count, width), LOW) for width in widths]
        + [pltpu.VMEM((count, depth), LOW), pltpu.SemaphoreType.DMA((5,))],
        smem=1,
        any_from=1,
        any_outs=(0, 1),
        after=after,
        cost=(2 * count * depth * sum(widths), 2 * count * depth + 2 * depth * sum(widths)),
    )


def summed(parts, at):
    total = parts[0][at, :]
    if len(parts) > 1:
        half = parts[1].shape[0]
        part = parts[1] if at.start < half else parts[2]
        first = at.start % half
        total = total + part[first : first + ROWS, :].astype(F32)
    return total


def row_steps(count):
    return [slice(first, first + ROWS) for first in range(0, count, ROWS)]


def inverse_rms(values):
    return lax.rsqrt(jnp.mean(values * values, axis=1, keepdims=True) + EPSILON)


def norm_kernel(tokens, gains, out):
    for at in row_steps(tokens.shape[0]):
        values = tokens[at, :].astype(F32)
        out[at, :] = (values * inverse_rms(values) * gains[...]).astype(LOW)


def residual_kernel(tokens, gains, squares, *refs):
    parts, (residual_out, ffn_out, inverse_out) = refs[:-3], refs[-3:]
    width = tokens.shape[1]
    for at in row_steps(tokens.shape[0]):
        inverse = lax.rsqrt(squares[at, :] * (1.0 / width) + EPSILON)
        inverse_out[at, :] = inverse
        residual = tokens[at, :].astype(F32) + summed(parts, at) * inverse
        residual_out[at, :] = residual
        ffn_out[at, :] = (residual * inverse_rms(residual) * gains[...]).astype(LOW)


def grad_residual_kernel(tokens, cotangent, gains, residual_in, inverse_in, *refs):
    parts, (grad_out, low_out) = refs[:-2], refs[-2:]
    width = tokens.shape[1]
    lane = lax.broadcasted_iota(jnp.int32, (ROWS, 128), 1)
    for at in row_steps(tokens.shape[0]):
        residual = residual_in[at, :]
        inverse = inverse_rms(residual)
        normed = residual * inverse
        grad_normed = summed(parts, at) * gains[...]
        mean = jnp.mean(grad_normed * normed, axis=1, keepdims=True)
        grad = cotangent[at, :].astype(F32) + inverse * (grad_normed - normed * mean)
        grad_out[at, :] = grad
        low = grad.astype(LOW)
        low_out[at, :width] = low
        branch = residual - tokens[at, :].astype(F32)
        factors = jnp.zeros((ROWS, 128), F32)
        for i, factor in enumerate(
            (inverse_in[at, :], jnp.mean(low.astype(F32) * branch, axis=1, keepdims=True))
        ):
            high = factor.astype(LOW).astype(F32)
            factors = jnp.where(lane == 2 * i, high, factors)
            factors = jnp.where(lane == 2 * i + 1, factor - high, factors)
        low_out[at, width:] = factors.astype(LOW)


def output_rows_kernel(residual, *refs):
    parts, out = refs[:-1], refs[-1]
    for at in row_steps(residual.shape[0]):
        out[at, :] = (residual[at, :] + summed(parts, at)).astype(LOW)


def grad_tokens_kernel(tokens, gains, grad_residual, *refs):
    parts, out = refs[:-1], refs[-1]
    for at in row_steps(tokens.shape[0]):
        values = tokens[at, :].astype(F32)
        inverse = inverse_rms(values)
        normed = values * inverse
        grad_normed = summed(parts, at) * gains[...]
        mean = jnp.mean(grad_normed * normed, axis=1, keepdims=True)
        out[at, :] = (
            grad_residual[at, :] + inverse * (grad_normed - normed * mean)
        ).astype(LOW)


def core_sum_kernel(rows, mine, other, top_out, end_out, top_keep, end_keep):
    half = rows // 2
    for x in range(2):
        for y in range(2):
            slot = x * 2 + y
            for first in range(0, rows, ROWS):
                at = slice(slot * rows + first, slot * rows + first + ROWS)
                total = mine[at, :].astype(F32) + other[at, :].astype(F32)
                low = total.astype(LOW)
                if first < half:
                    if x:
                        top_out[y * half + first : y * half + first + ROWS, :] = low
                    else:
                        top_keep[y * half + first : y * half + first + ROWS, :] = low
                else:
                    to = x * half + first - half
                    if y:
                        end_out[to : to + ROWS, :] = low
                    else:
                        end_keep[to : to + ROWS, :] = low


def chip_sum_kernel(top, end, top_in, end_in, top_out, end_out, keep):
    half = top.shape[0] // 2
    for i, (mine, other, out) in enumerate(((top, top_in, top_out), (end, end_in, end_out))):
        for first in range(0, half, ROWS):
            at = slice(first, first + ROWS)
            keep[i * half + first : i * half + first + ROWS, :] = mine[at, :].astype(
                F32
            ) + other[at, :].astype(F32)
            at = slice(half + first, half + first + ROWS)
            out[first : first + ROWS, :] = (
                mine[at, :].astype(F32) + other[at, :].astype(F32)
            ).astype(LOW)


class Links:
    def __init__(self, sizes):
        self.sizes = sizes
        self.pairs = sizes["y"] == sizes["core"] == sizes["x"] == 2
        self.plane = ("x", "y", "core")
        self.owners = ("y", "core", "x")

    def place(self, axis):
        return lax.axis_index(axis)

    def slots(self):
        sizes = self.sizes
        x, y, core = jnp.meshgrid(
            jnp.arange(sizes["x"]), jnp.arange(sizes["y"]), jnp.arange(sizes["core"]), indexing="ij"
        )
        if self.pairs:
            x, y, core = x ^ self.place("x"), y ^ self.place("y"), core ^ self.place("core")
            slot = (core * 2 + x) * 2 + y
        else:
            slot = (x * sizes["y"] + y) * sizes["core"] + core
        return slot.reshape(-1).astype(jnp.int32)

    def swap(self, axis, value):
        return lax.ppermute(value, axis, SWAP)

    def rows(self, value, after=()):
        if not self.pairs:
            return [lax.all_gather(value, self.plane, axis=0, tiled=True)]
        half = value.shape[0] // 2
        by_x, by_y = self.swap("x", value), self.swap("y", value)
        top, end = call(
            halves_kernel, "halves", [((half, value.shape[1]), LOW)] * 2, [by_x, by_y], after=after
        )
        own = [value, by_y, by_x, self.swap("y", top), self.swap("x", end)]
        return own + [self.swap("core", piece) for piece in own]

    def sum_cores(self, parts, after=()):
        if not self.pairs:
            return parts
        away, mine = parts
        rows, width = mine.shape[0] // 4, mine.shape[1]
        return call(
            functools.partial(core_sum_kernel, rows),
            "core_sum",
            [((rows, width), LOW)] * 4,
            [mine, self.swap("core", away)],
            cost=(8 * rows * width, 24 * rows * width),
            after=after,
        )

    def sum_chips(self, parts, after=()):
        if not self.pairs:
            return [
                lax.psum_scatter(parts[0], self.plane, scatter_dimension=0, tiled=True).astype(F32)
            ]
        top, end, top_keep, end_keep = parts
        rows, width = top.shape
        top, end, keep = call(
            chip_sum_kernel,
            "chip_sum",
            [((rows // 2, width), LOW)] * 2 + [((rows, width), F32)],
            [top_keep, end_keep, self.swap("x", top), self.swap("y", end)],
            cost=(2 * rows * width, 12 * rows * width),
            after=after,
        )
        return [keep, self.swap("y", top), self.swap("x", end)]

    def sum_rows_small(self, parts):
        parts = lax.all_to_all(parts, self.plane, split_axis=0, concat_axis=0, tiled=True)
        return jnp.sum(parts, axis=0)

    def sum_planes_small(self, value):
        planes = self.sizes["z"]
        if not (self.pairs and planes & (planes - 1) == 0):
            return lax.psum(value, "z")
        step = 1
        while step < planes:
            value = value + lax.ppermute(value, "z", [(i, i ^ step) for i in range(planes)])
            step *= 2
        return value

    def sum_plane_small(self, value):
        if not self.pairs:
            return lax.psum(value, self.plane)
        for axis in ("x", "y", "core"):
            value = value + self.swap(axis, value)
        return value

    def exchange(self, value):
        return lax.all_to_all(value, self.owners, split_axis=0, concat_axis=0, tiled=True)

    def ring(self, value):
        planes = self.sizes["z"]

        def shift(value, by):
            return lax.ppermute(value, "z", [(i, (i + by) % planes) for i in range(planes)])

        up, down = [value], []
        while 1 + len(up) + len(down) <= planes:
            up.append(shift(up[-1], 1))
            if 1 + len(up) + len(down) <= planes:
                down.insert(0, shift(down[0] if down else value, -1))
        return up + down

    def sum_planes(self, value):
        return lax.psum_scatter(value, "z", scatter_dimension=0, tiled=True)

    def both_x(self, value):
        if self.sizes["x"] == 1:
            return value
        if self.sizes["x"] != 2:
            return lax.all_gather(value, "x", axis=0, tiled=True)
        other = self.swap("x", value)
        return jnp.where(
            self.place("x") == 0,
            jnp.concatenate([value, other], axis=0),
            jnp.concatenate([other, value], axis=0),
        )


def on_device(
    sizes,
    tokens,
    doc_lengths,
    w_in,
    w_forget,
    w_gate_out,
    w_out,
    w_gate,
    w_up,
    w_down,
    g_mix,
    g_out,
    g_ffn,
    floor_logit,
    cotangent,
):
    links = Links(sizes)
    tokens, cotangent = tokens[0], cotangent[0]
    row_count, width = tokens.shape
    block = w_in.shape[0]
    hidden = w_gate.shape[1]
    layout = Layout(sizes, row_count, block, hidden)
    seq, planes, buckets, parts = layout.seq, layout.planes, layout.buckets, layout.parts
    slab = width // parts
    seq_place = links.place("y") * sizes["core"] + links.place("core")
    x_place, z_place = links.place("x"), links.place("z")
    owner = (seq_place * planes + z_place) * buckets + x_place
    place = z_place.astype(jnp.int32).reshape(1)
    wide, low_wide = ((row_count, width), F32), ((row_count, width), LOW)
    column = ((row_count, 1), F32)
    row_cost = (20 * row_count * width, 8 * row_count * width)

    def own_channels(vector):
        return lax.dynamic_index_in_dim(
            lax.dynamic_index_in_dim(
                vector.reshape(-1, seq, planes, buckets, block), seq_place, 1, keepdims=False
            ),
            x_place,
            2,
            keepdims=False,
        ).reshape(-1, slab)

    def to_hidden(first, size, after):
        return call(
            functools.partial(to_hidden_kernel, layout, first, size),
            "to_hidden",
            [((parts, block, -(-3 * size // 128) * 128), LOW)],
            [w_gate, w_up, w_down],
            after=after,
        )[0]

    def gather_weights(weight, ring=True):
        weight = weight.reshape(parts * block, -1)
        if layout.pieces and ring:
            return links.ring(weight)
        if layout.pieces:
            return [lax.all_gather(weight, "z", axis=0, tiled=True)]
        full = lax.all_gather(weight, "z", axis=0)
        full = full.reshape(planes, seq, layout.strip, -1)
        return [jnp.swapaxes(full, 0, 1).reshape(width, -1)]

    def gather_channels(weight):
        if layout.pieces:
            return links.ring(weight)
        return [lax.all_gather(weight, "z", axis=0, tiled=True)]

    def scatter_weights(grads):
        if not layout.pieces:
            grads = grads.reshape(seq, planes, layout.strip, -1)
            grads = jnp.swapaxes(grads, 0, 1).reshape(width, -1)
        return links.sum_planes(grads).reshape(parts, block, -1)

    (mixer,) = call(
        functools.partial(to_channels_kernel, layout),
        "to_channels",
        [((parts, block, 3 * slab), LOW)],
        [w_in, w_forget, w_gate_out],
    )
    vectors = jnp.stack([g_mix, g_ffn, g_out, floor_logit]).astype(F32)
    vectors = links.sum_planes_small(
        lax.dynamic_update_slice(jnp.zeros((4, width), F32), vectors, (0, owner * block))
    )
    mixer = gather_weights(hold(links.exchange(mixer), [vectors]))
    vectors = links.sum_plane_small(vectors)
    out_weights = [lax.all_gather(w_out, "z", axis=0, tiled=True)]
    gain_mix, gain_ffn = vectors[0:1], vectors[1:2]
    own_vectors = own_channels(vectors[2:])
    gain_out = own_vectors[0:1]
    floors = jax.nn.sigmoid(own_vectors[1:2])
    slots = links.slots()
    ends = links.both_x(jnp.cumsum(doc_lengths, axis=1).astype(jnp.int32))

    (mixed,) = call(
        norm_kernel, "mixed_in", [low_wide], [tokens, gain_mix], cost=row_cost
    )
    first = links.exchange(to_hidden(0, layout.split, [mixed, *out_weights]))
    mixed = links.rows(mixed)
    first = gather_weights(hold(first, [*mixer[1:2], *mixer[-1:], *mixed[3:5]]), False)
    second = links.exchange(to_hidden(layout.split, layout.rest, mixer[1:2] + mixer[-1:]))
    early = [second]
    second = gather_weights(second, False)
    grads_all = links.rows(hold(cotangent, early))
    forget, floor_term, slope_forget, slope_input, gate_pre, states, scaled, squares = (
        mixer_forward(layout, slots, ends, place, floors, gain_out, mixed, mixer, early)
    )
    squares = links.sum_rows_small(squares).reshape(row_count, 1)
    branch = branch_parts(layout, place, scaled, out_weights, grads_all[1:3])
    branch = links.sum_cores(branch, grads_all[3:5])
    branch = links.sum_chips(branch)
    residual, ffn, inverse_h = call(
        residual_kernel,
        "residual",
        [wide, low_wide, column],
        [tokens, gain_ffn, squares, *branch],
        cost=row_cost,
    )

    ffn = links.rows(ffn)
    first_acts, first_grads = glu_first(layout, place, ffn, grads_all, first)
    first_grads = scatter_weights(first_grads)
    second_acts, *ffn_parts = glu_second(
        layout, place, ffn, grads_all, first, second, first_acts
    )
    ffn_parts = links.sum_cores(ffn_parts)
    second_grads = glu_third(layout, place, ffn, grads_all, second_acts, [])
    grad_ffn = links.sum_chips(ffn_parts, [second_grads])
    second_grads = scatter_weights(second_grads)
    grad_residual, grad_low = call(
        grad_residual_kernel,
        "grad_residual",
        [wide, ((row_count, width + 128), LOW)],
        [tokens, cotangent, gain_ffn, residual, inverse_h, *grad_ffn],
        cost=row_cost,
    )
    out_parts = output_parts(
        layout, place, first, second, first_acts, second_acts, width, []
    )

    grads_low = links.rows(grad_low, out_parts[:1])
    saved = [gate_pre, states, forget, floor_term, slope_forget, slope_input]
    mixer_grads, out_grads, mixer_weight_grads = mixer_backward(
        layout,
        slots,
        place,
        gain_out,
        saved,
        grads_low,
        out_weights,
        mixed,
        [],
    )
    mixer_weight_grads = scatter_weights(mixer_weight_grads)
    out_grads = links.sum_planes(out_grads)
    mixed_parts = links.sum_cores(
        mixed_grad_parts(layout, place, mixer_grads, mixer, width, [])
    )
    grad_mixed = links.sum_chips(mixed_parts)
    (grad_tokens,) = call(
        grad_tokens_kernel,
        "grad_tokens",
        [low_wide],
        [tokens, gain_mix, grad_residual, *grad_mixed],
        cost=row_cost,
    )
    output = links.sum_chips(links.sum_cores(out_parts, [grad_tokens]))
    (output,) = call(
        output_rows_kernel, "output_rows", [low_wide], [residual, *output], cost=row_cost
    )
    first_grads = links.exchange(hold(first_grads, [grad_tokens]))
    second_grads = links.exchange(hold(second_grads, [output]))
    mixer_weight_grads = links.exchange(mixer_weight_grads)

    def as_column(vector):
        return vector.astype(F32).reshape(block, 1)

    square, long, single = ((block, width), F32), ((block, hidden), F32), ((block, 1), F32)
    gate_w, up_w, down_w, grad_g_ffn = call(
        functools.partial(from_hidden_kernel, layout),
        "from_hidden",
        [long] * 3 + [single],
        [first_grads, second_grads, as_column(g_ffn), w_gate, w_up],
    )
    out_w, grad_g_out, grad_floor = call(
        channel_gain_kernel,
        "from_out",
        [square, single, single],
        [out_grads, w_out, as_column(g_out), as_column(floor_logit)],
    )
    in_w, forget_w, gate_out_w, grad_g_mix = call(
        functools.partial(from_channels_kernel, layout),
        "from_channels",
        [square] * 3 + [single],
        [mixer_weight_grads, as_column(g_mix), w_in, w_forget, w_gate_out],
    )
    return (
        output[None],
        grad_tokens[None],
        in_w,
        forget_w,
        gate_out_w,
        out_w,
        gate_w,
        up_w,
        down_w,
        grad_g_mix.reshape(block),
        grad_g_out.reshape(block),
        grad_g_ffn.reshape(block),
        grad_floor.reshape(block),
    )


def solution(mesh):
    seq, dp = mesh.shape["seq"], mesh.shape["dp"]
    core = 2 if seq % 2 == 0 else 1
    x = max(1, TENSOR_PARTS // seq)
    if dp % x:
        x = 1
    sizes = {"y": seq // core, "core": core, "z": dp // x, "x": x}
    split = Mesh(mesh.devices.reshape(tuple(sizes.values())), tuple(sizes))
    rows = P(("z", "x"), ("y", "core"), None)
    lengths = P(("z", "x"), None)
    matrix = P(("y", "core", "z", "x"), None)
    vector = P(("y", "core", "z", "x"))
    return jax.shard_map(
        functools.partial(on_device, sizes),
        mesh=split,
        in_specs=(rows, lengths) + (matrix,) * 7 + (vector,) * 4 + (rows,),
        out_specs=(rows, rows) + (matrix,) * 7 + (vector,) * 4,
        check_vma=False,
    )
```

```python
import functools
import math

import jax
import jax.numpy as jnp
from jax import lax
from jax.experimental import pallas as pl
from jax.experimental.pallas import tpu as pltpu
from jax.sharding import Mesh
from jax.sharding import PartitionSpec as P

EPSILON = 1e-06
F32 = jnp.float32
LOW = jnp.bfloat16
TENSOR_PARTS = 8
SWAP = [(0, 1), (1, 0)]
ROWS = 16
TILE = 512
SLOTS = 2
COST = 1
VMEM_BYTES = 58 * 1024 * 1024
SPARE_BYTES = 12 * 1024 * 1024
VMEM_SPEC = pl.BlockSpec(memory_space=pltpu.VMEM)
TOKEN = ((8, 128), F32)
SMEM_SPEC = pl.BlockSpec(memory_space=pltpu.SMEM)
ANY_SPEC = pl.BlockSpec(memory_space=pl.ANY)


def product(left_op, right_op):
    return jnp.dot(left_op, right_op, preferred_element_type=F32)


def product_nt(left_op, right_op):
    return lax.dot_general(
        left_op, right_op, (((1,), (1,)), ((), ())), preferred_element_type=F32
    )


def product_tn(left_op, right_op):
    return lax.dot_general(
        left_op, right_op, (((0,), (0,)), ((), ())), preferred_element_type=F32
    )


def call(
    kernel,
    name,
    outs,
    operands,
    scratch=(),
    smem=0,
    any_from=None,
    any_outs=(),
    cost=(0, 0),
    after=(),
    token=False,
):
    any_from = len(operands) if any_from is None else any_from
    if after:
        inner, count, extra = kernel, len(operands), len(after)

        def kernel(*refs):
            inner(*refs[:count], *refs[count + extra :])

        operands = list(operands) + list(after)
        any_from = min(any_from, count)
    if token:
        plain, mark = kernel, len(operands) + len(outs)

        def kernel(*refs):
            refs[mark][...] = jnp.zeros(TOKEN[0], F32)
            plain(*refs[:mark], *refs[mark + 1 :])

        any_outs = [i for i in any_outs if i < len(outs)]
        outs = list(outs) + [TOKEN]
    held = list(operands[smem:any_from]) + [
        jax.ShapeDtypeStruct(*out) for i, out in enumerate(outs) if i not in any_outs
    ]
    held = sum(math.prod(array.shape) * array.dtype.itemsize for array in held)
    specs = [
        SMEM_SPEC if i < smem else (ANY_SPEC if i >= any_from else VMEM_SPEC)
        for i in range(len(operands))
    ]
    return pl.pallas_call(
        kernel,
        out_shape=tuple(jax.ShapeDtypeStruct(*out) for out in outs),
        in_specs=specs,
        out_specs=tuple(ANY_SPEC if i in any_outs else VMEM_SPEC for i in range(len(outs))),
        scratch_shapes=list(scratch),
        compiler_params=pltpu.CompilerParams(
            vmem_limit_bytes=VMEM_BYTES if scratch else held + SPARE_BYTES
        ),
        cost_estimate=pl.CostEstimate(
            flops=int(cost[0] * COST), bytes_accessed=int(cost[1] * COST), transcendentals=0
        ),
        name=name,
    )(*operands)


def await_copies(view, sem):
    pltpu.make_async_copy(view, view, sem).wait()


def send(source, target, sem):
    pltpu.make_async_copy(source, target, sem).start()


class Layout:
    def __init__(self, sizes, slot_rows, block, hidden):
        self.seq = sizes["y"] * sizes["core"]
        self.planes = sizes["z"]
        self.buckets = sizes["x"]
        self.parts = self.seq * self.buckets
        self.slot_rows = slot_rows
        self.block = block
        share = hidden // self.parts
        self.split = -(-share // 256) * 128
        self.rest = share - self.split
        self.pieces = sizes["y"] == sizes["core"] == sizes["x"] == 2
        self.strip = self.buckets * block
        half = slot_rows // 2
        self.row_pieces = (
            [(c + s, r) for c in (0, 4) for s, r in ((0, 0), (1, 0), (2, 0), (3, 0), (3, half))]
            if self.pieces
            else [(0, 0)]
        )
        self.row_count = len(self.row_pieces)
        self.plane_count = self.planes if self.pieces else 1
        self.step_rows = SLOTS * slot_rows
        self.steps = self.parts // SLOTS

    def step(self, index):
        return pl.ds(pl.multiple_of(index * self.step_rows, self.step_rows), self.step_rows)

    def await_step(self, target, sems, index):
        for i in range(SLOTS):
            slot = index * SLOTS + i
            first = pl.multiple_of(slot * self.slot_rows, self.slot_rows)
            await_copies(target.at[pl.ds(first, self.slot_rows)], sems.at[slot])

    def fill_rows(self, pieces, target, sems):
        if not self.pieces:
            for slot in range(self.parts):
                at = pl.ds(slot * self.slot_rows, self.slot_rows)
                send(pieces[0].at[at], target.at[at], sems.at[slot])
            return
        for piece, (slot, first) in zip(pieces, self.row_pieces):
            at = pl.ds(slot * self.slot_rows + first, piece.shape[0])
            send(piece, target.at[at], sems.at[slot])

    def fill_weights(self, place, pieces, target, sem, columns=None):
        columns = target.shape[1] if columns is None else columns
        lanes = pl.ds(0, columns)
        if not self.pieces:
            send(pieces[0].at[:, lanes], target, sem)
            return
        if len(pieces) == 1:
            for plane in range(self.planes):
                for s in range(self.seq):
                    send(
                        pieces[0].at[pl.ds((plane * self.seq + s) * self.strip, self.strip), lanes],
                        target.at[pl.ds((s * self.planes + plane) * self.strip, self.strip)],
                        sem,
                    )
            return
        for step, piece in enumerate(pieces):
            plane = lax.rem(place - step + self.planes, self.planes)
            for s in range(self.seq):
                first = pl.multiple_of((s * self.planes + plane) * self.strip, self.strip)
                send(
                    piece.at[pl.ds(s * self.strip, self.strip), lanes],
                    target.at[pl.ds(first, self.strip)],
                    sem,
                )

    def fill_channels(self, place, pieces, target, sem):
        if len(pieces) == 1:
            send(pieces[0], target, sem)
            return
        for step, piece in enumerate(pieces):
            plane = lax.rem(place - step + self.planes, self.planes)
            first = pl.multiple_of(plane * self.block, self.block)
            send(piece, target.at[pl.ds(first, self.block)], sem)

    def strip_row(self, index):
        if not self.pieces:
            return index * self.strip
        return pl.multiple_of(
            ((index % self.planes) * self.seq + index // self.planes) * self.strip, self.strip
        )

    def weight_grads(self, out, staged, sem, step, value):
        if not self.pieces:
            rows = pl.ds(pl.multiple_of(step * TILE, TILE), TILE)
            staged[rows, :] = value
            send(staged.at[rows], out.at[rows], sem)
            return
        per = TILE // self.strip
        for i in range(per):
            rows = pl.ds(self.strip_row(step * per + i), self.strip)
            staged[rows, :] = value[i * self.strip : (i + 1) * self.strip]
            send(staged.at[rows], out.at[rows], sem)


def to_channels_kernel(layout, *refs):
    *weights, out = refs
    block, width = layout.block, layout.block * layout.planes
    for i, weight in enumerate(weights):
        for s in range(layout.seq):
            for z in range(layout.planes):
                for x in range(layout.buckets):
                    first = ((s * layout.planes + z) * layout.buckets + x) * block
                    to = i * width + z * block
                    out[s * layout.buckets + x, :, to : to + block] = weight[
                        :, first : first + block
                    ]


def from_channels_kernel(layout, grads, gains, *refs):
    count = (len(refs) - 1) // 2
    weights, outs, gain_out = refs[:count], refs[count:-1], refs[-1]
    block, width = layout.block, layout.block * layout.planes
    total = jnp.zeros((block, 1), F32)
    for i, (weight, out) in enumerate(zip(weights, outs)):
        for s in range(layout.seq):
            for z in range(layout.planes):
                for x in range(layout.buckets):
                    first = ((s * layout.planes + z) * layout.buckets + x) * block
                    at = i * width + z * block
                    out[:, first : first + block] = grads[
                        s * layout.buckets + x, :, at : at + block
                    ].astype(F32)
        total = total + jnp.sum(out[...] * weight[...].astype(F32), axis=1, keepdims=True)
    gain_out[...] = total / gains[...]


def to_hidden_kernel(layout, first, size, *refs):
    *weights, out = refs
    share = weights[0].shape[1] // layout.parts
    for i, weight in enumerate(weights):
        for part in range(layout.parts):
            at = part * share + first
            out[part, :, i * size : (i + 1) * size] = weight[:, at : at + size]
    used = len(weights) * size
    if used < out.shape[2]:
        out[:, :, used:] = jnp.zeros((layout.parts, layout.block, out.shape[2] - used), LOW)


def from_hidden_kernel(layout, first, second, gains, *refs):
    *weights, gate_out, up_out, down_out, gain_out = refs
    split, rest = layout.split, layout.rest
    share = split + rest
    total = jnp.zeros((layout.block, 1), F32)
    for i, out in enumerate((gate_out, up_out, down_out)):
        for part in range(layout.parts):
            at = part * share
            out[:, at : at + split] = first[part, :, i * split : (i + 1) * split].astype(F32)
            out[:, at + split : at + share] = second[part, :, i * rest : (i + 1) * rest].astype(F32)
        if i < len(weights):
            total = total + jnp.sum(out[...] * weights[i][...].astype(F32), axis=1, keepdims=True)
    gain_out[...] = total / gains[...]


def channel_gain_kernel(grads, weight, gains, floors, out, gain_out, floor_out):
    width = weight.shape[1]
    out[...] = grads[:, :width].astype(F32)
    total = jnp.sum(out[...] * weight[...].astype(F32), axis=1, keepdims=True)
    gain_out[...] = total / gains[...]
    floor = jax.nn.sigmoid(floors[...])
    floor_out[...] = grads[:, width : width + 1].astype(F32) * floor * (1.0 - floor)


def hold_kernel(value, out):
    out[...] = value[...]


def hold(value, after):
    return call(hold_kernel, "hold", [(value.shape, value.dtype)], [value], after=after)[0]


def pin_kernel(value, *refs):
    del value, refs


def pin(value, after):
    return pl.pallas_call(
        pin_kernel,
        out_shape=jax.ShapeDtypeStruct(value.shape, value.dtype),
        in_specs=[ANY_SPEC] * (1 + len(after)),
        out_specs=ANY_SPEC,
        input_output_aliases={0: 0},
        name="pin",
    )(value, *after)


def halves_kernel(by_x, by_y, top, end):
    half = top.shape[0]
    top[...] = by_x[:half, :]
    end[...] = by_y[half:, :]


def row_marks(ends, bucket, first, shape):
    rows = first + lax.broadcasted_iota(jnp.int32, shape, 0)
    docs = ends.shape[1]
    hit = rows == 0
    for doc in range(docs - 1):
        hit = jnp.logical_or(hit, rows == ends[bucket, doc])
    keep = jnp.where(hit, 0.0, 1.0)
    live = jnp.where(rows < ends[bucket, docs - 1], 1.0, 0.0)
    return (keep, live)


def prefix(decay, term, forward):
    rows = lax.broadcasted_iota(jnp.int32, decay.shape, 0)
    for step in (1, 2, 4):
        shift = step if forward else 8 - step
        inside = rows >= step if forward else rows < 8 - step
        moved_term = jnp.where(inside, pltpu.roll(term, shift, 0), 0.0)
        moved_decay = jnp.where(inside, pltpu.roll(decay, shift, 0), 1.0)
        term = term + decay * moved_term
        decay = decay * moved_decay
    return (decay, term)


def mixer_forward_kernel(
    layout,
    slots,
    ends,
    place,
    floors,
    gains,
    *refs,
):
    rows_in = refs[: layout.row_count]
    weights_in = refs[layout.row_count : layout.row_count + layout.plane_count]
    outs, refs = refs[layout.row_count + layout.plane_count :][:7], refs[-13:]
    rows_ref, weights, pre, row_sems, weight_sem, out_sems, *kept = refs
    (
        forget_out,
        floor_out,
        slope_forget_out,
        slope_input_out,
        gate_out,
        states_out,
        scaled_out,
    ) = kept
    width = floors.shape[1]
    seg_rows = layout.slot_rows
    buckets, segments = layout.buckets, layout.seq
    layout.fill_weights(place[0], weights_in, weights, weight_sem)
    layout.fill_rows(rows_in, rows_ref, row_sems)
    await_copies(weights, weight_sem)

    def multiply(step, _):
        at = layout.step(step)
        layout.await_step(rows_ref, row_sems, step)
        pre[at, :] = product(rows_ref[at, :], weights[...])
        return 0

    lax.fori_loop(0, layout.steps, multiply, 0)
    floor = floors[...]
    gain = gains[...]
    first_row = lax.broadcasted_iota(jnp.int32, (8, width), 0) == 0

    def one(bucket, segment, block, carry):
        base = pl.multiple_of(slots[bucket * segments + segment] * seg_rows + block * ROWS, ROWS)
        at = pl.ds(base, ROWS)
        keep, live = row_marks(ends, bucket, segment * seg_rows + block * ROWS, (ROWS, width))
        input_pre = pre[at, :width].astype(LOW).astype(F32)
        forget_pre = pre[at, width : 2 * width].astype(LOW).astype(F32)
        gate_pre = pre[at, 2 * width :]
        gate_out[at, :] = gate_pre
        sig_forget = jax.nn.sigmoid(forget_pre)
        forget = (floor + (1.0 - floor) * sig_forget) * keep
        sig_input = jax.nn.sigmoid(input_pre)
        drive = input_pre * sig_input * live
        term = (1.0 - forget) * drive
        hidden, previous = [], []
        for low in range(0, ROWS, 8):
            decay_part, term_part = prefix(forget[low : low + 8], term[low : low + 8], True)
            here = term_part + decay_part * carry
            previous.append(jnp.where(first_row, carry, pltpu.roll(here, 1, 0)))
            hidden.append(here)
            carry = here[7:8]
        hidden = jnp.concatenate(hidden, axis=0)
        previous = jnp.concatenate(previous, axis=0)
        forget_out[at, :] = forget
        floor_term = (previous - drive) * keep * (1.0 - sig_forget)
        floor_out[at, :] = floor_term
        slope_forget_out[at, :] = floor_term * (1.0 - floor) * sig_forget
        slope_input_out[at, :] = (
            (1.0 - forget) * live * (sig_input * (1.0 + input_pre * (1.0 - sig_input)))
        )
        states = hidden.astype(LOW)
        states_out[at, :] = states
        scaled_out[at, :] = (
            states.astype(F32) * gain * (gate_pre * jax.nn.sigmoid(gate_pre))
        ).astype(LOW)
        return carry

    def over_segments(segment, carries):
        def over_blocks(block, carries):
            return tuple(one(b, segment, block, carries[b]) for b in range(buckets))

        carries = lax.fori_loop(0, seg_rows // ROWS, over_blocks, carries)
        for b in range(buckets):
            first = pl.multiple_of(slots[b * segments + segment] * seg_rows, seg_rows)
            at = pl.ds(first, seg_rows)
            for i, (ref, out) in enumerate(zip(kept, outs)):
                send(ref.at[at], out.at[at], out_sems.at[i])
        return carries

    lax.fori_loop(
        0, segments, over_segments, tuple(jnp.zeros((1, width), F32) for _ in range(buckets))
    )
    for i, ref in enumerate(kept):
        await_copies(ref, out_sems.at[i])


def mixer_forward(layout, slots, ends, place, floors, gains, rows, weights, after):
    count = layout.parts * layout.slot_rows
    width = floors.shape[1]
    depth = rows[0].shape[1]
    wide = (count, width)
    return call(
        functools.partial(mixer_forward_kernel, layout),
        "mixer_forward",
        [(wide, F32)] * 5 + [(wide, LOW)] * 2,
        [slots, ends, place, floors, gains, *rows, *weights],
        [
            pltpu.VMEM((count, depth), LOW),
            pltpu.VMEM((depth, 3 * width), LOW),
            pltpu.VMEM((count, 3 * width), F32),
            pltpu.SemaphoreType.DMA((layout.parts,)),
            pltpu.SemaphoreType.DMA,
            pltpu.SemaphoreType.DMA((7,)),
        ]
        + [pltpu.VMEM(wide, F32)] * 5
        + [pltpu.VMEM(wide, LOW)] * 2,
        smem=3,
        any_from=5,
        any_outs=tuple(range(7)),
        after=after,
        cost=(6 * count * width * depth, 2 * count * depth + 6 * depth * width + 24 * count * width),
    )


def split_lanes(*columns):
    shape = (columns[0].shape[0], 128)
    lane = lax.broadcasted_iota(jnp.int32, shape, 1)
    lanes = jnp.zeros(shape, F32)
    for i, column in enumerate(columns):
        high = column.astype(LOW).astype(F32)
        lanes = jnp.where(lane == 2 * i, high, lanes)
        lanes = jnp.where(lane == 2 * i + 1, column - high, lanes)
    return lanes.astype(LOW)


def branch_kernel(layout, place, scaled, states, *refs):
    weights_in = refs[:1]
    outs = refs[1:-4]
    weights, staged, sem, out_sem = refs[-4:]
    layout.fill_channels(place[0], weights_in, weights, sem)
    await_copies(weights, sem)

    def rows_of(at):
        values = states[at, :].astype(F32)
        squares = jnp.sum(values * values, axis=1, keepdims=True)
        parts = product(scaled[at, :], weights[...]).astype(LOW)
        return jnp.concatenate([parts, split_lanes(squares)], axis=1)

    write_parts(layout, outs, staged, out_sem, rows_of)
    await_copies(staged, out_sem)


def write_parts(layout, outs, staged, sem, rows_of):
    per = layout.steps // len(outs)
    for i, out in enumerate(outs):
        start = (len(outs) - 1 - i) * per

        def one(step, _):
            at = layout.step(start + step)
            staged[at, :] = rows_of(at).astype(LOW)
            send(staged.at[at], out.at[layout.step(step)], sem)
            return 0

        lax.fori_loop(0, per, one, 0)


def part_shapes(layout, width):
    count = layout.parts * layout.slot_rows
    if layout.pieces:
        return [((count // 2, width), LOW)] * 2
    return [((count, width), LOW)]


def branch_parts(layout, place, scaled, states, weights, after):
    count, channels = scaled.shape
    width = weights[0].shape[1]
    return call(
        functools.partial(branch_kernel, layout),
        "branch_parts",
        part_shapes(layout, width + 128),
        [place, scaled, states, *weights],
        [
            pltpu.VMEM((channels, width), LOW),
            pltpu.VMEM((count, width + 128), LOW),
            pltpu.SemaphoreType.DMA,
            pltpu.SemaphoreType.DMA,
        ],
        smem=1,
        any_from=3,
        any_outs=(0, 1),
        after=after,
        cost=(2 * count * channels * width, 2 * count * width + 2 * channels * width),
    )


def mixer_backward_kernel(
    layout,
    slots,
    place,
    gains,
    *refs,
):
    saved, refs = refs[:6], refs[6:]
    rows_in = refs[: layout.row_count]
    refs = refs[layout.row_count :]
    weights_in, refs = refs[:1], refs[1:]
    mixed_in, refs = refs[: layout.row_count], refs[layout.row_count :]
    (
        grads_out,
        out_grads,
        mixer_grads,
        rows_ref,
        weights,
        mixed,
        grad_branch,
        branch,
        staged_out,
        staged,
        row_sems,
        weight_sem,
        mixed_sems,
        out_sems,
        saved_sems,
        *kept,
    ) = refs
    gate_in, states_in, forget_in, floor_in, slope_forget_in, slope_input_in = kept
    width = gains.shape[1]
    depth = weights.shape[1]
    seg_rows = layout.slot_rows
    buckets, segments = layout.buckets, layout.seq
    layout.fill_channels(place[0], weights_in, weights, weight_sem)
    layout.fill_rows(rows_in, rows_ref, row_sems)
    for i, (source, target) in enumerate(zip(saved, kept)):
        send(source, target, saved_sems.at[i])
    layout.fill_rows(mixed_in, mixed, mixed_sems)
    await_copies(weights, weight_sem)

    def multiply(step, _):
        at = layout.step(step)
        layout.await_step(rows_ref, row_sems, step)
        grad_branch[at, :] = product_nt(rows_ref[at, :depth], weights[...])
        return 0

    lax.fori_loop(0, layout.steps, multiply, 0)
    for i, target in enumerate(kept):
        await_copies(target, saved_sems.at[i])
    gain = gains[...]
    last_row = lax.broadcasted_iota(jnp.int32, (8, width), 0) == 7

    def one(bucket, segment, block, carry, floor_sum):
        base = pl.multiple_of(slots[bucket * segments + segment] * seg_rows + block * ROWS, ROWS)
        at = pl.ds(base, ROWS)
        grad_in = grad_branch[at, :]
        gate_pre = gate_in[at, :]
        factors = rows_ref[at, depth : depth + 4].astype(F32)
        inverse = factors[:, 0:1] + factors[:, 1:2]
        mean = factors[:, 2:3] + factors[:, 3:4]
        normed = states_in[at, :].astype(F32) * inverse
        sig_gate = jax.nn.sigmoid(gate_pre)
        silu_gate = gate_pre * sig_gate
        scaled = normed * gain
        branch[at, :] = (scaled * silu_gate).astype(LOW)
        grads_out[at, 2 * width :] = (
            grad_in * scaled * (sig_gate * (1.0 + gate_pre * (1.0 - sig_gate)))
        ).astype(LOW)
        grad_scaled = grad_in * silu_gate
        grad_hidden = (inverse * (grad_scaled * gain - normed * mean)).astype(LOW).astype(F32)
        forget = forget_in[at, :]
        term = forget * grad_hidden
        later = []
        for low in reversed(range(0, ROWS, 8)):
            decay_part, term_part = prefix(forget[low : low + 8], term[low : low + 8], False)
            here = term_part + decay_part * carry
            later.insert(0, jnp.where(last_row, carry, pltpu.roll(here, 7, 0)))
            carry = here[0:1]
        grad_total = grad_hidden + jnp.concatenate(later, axis=0)
        grads_out[at, :width] = (grad_total * slope_input_in[at, :]).astype(LOW)
        grads_out[at, width : 2 * width] = (grad_total * slope_forget_in[at, :]).astype(LOW)
        floor_sum = floor_sum + grad_total * floor_in[at, :]
        return (carry, floor_sum)

    def over_segments(step, state):
        segment = segments - 1 - step

        def over_blocks(block_step, state):
            block = seg_rows // ROWS - 1 - block_step
            carries, floor_sum = state
            fresh = []
            for b in range(buckets):
                carry, floor_sum = one(b, segment, block, carries[b], floor_sum)
                fresh.append(carry)
            return (tuple(fresh), floor_sum)

        return lax.fori_loop(0, seg_rows // ROWS, over_blocks, state)

    zeros = jnp.zeros((ROWS, width), F32)
    carries = tuple(jnp.zeros((1, width), F32) for _ in range(buckets))
    _, floor_sum = lax.fori_loop(0, segments, over_segments, (carries, zeros))
    staged_out[:, :depth] = product_tn(branch[...], rows_ref[:, :depth]).astype(LOW)
    ones = jnp.ones((ROWS, 128), LOW)
    high = floor_sum.astype(LOW)
    rest = (floor_sum - high.astype(F32)).astype(LOW)
    staged_out[:, depth:] = (product_tn(high, ones) + product_tn(rest, ones)).astype(LOW)
    send(staged_out, out_grads, out_sems.at[0])
    for slot in range(layout.parts):
        at = pl.ds(slot * seg_rows, seg_rows)
        await_copies(mixed.at[at], mixed_sems.at[slot])

    def over_features(step, _):
        columns = pl.ds(pl.multiple_of(step * TILE, TILE), TILE)
        value = product_tn(mixed[:, columns], grads_out[...]).astype(LOW)
        layout.weight_grads(mixer_grads, staged, out_sems.at[1], step, value)
        return 0

    lax.fori_loop(0, mixed.shape[1] // TILE, over_features, 0)
    await_copies(staged_out, out_sems.at[0])
    await_copies(staged, out_sems.at[1])


def mixer_backward(layout, slots, place, gains, saved, rows, weights, mixed, after):
    count = layout.parts * layout.slot_rows
    width = gains.shape[1]
    depth = mixed[0].shape[1]
    wide = depth + 128
    return call(
        functools.partial(mixer_backward_kernel, layout),
        "mixer_backward",
        [
            ((count, 3 * width), LOW),
            ((width, wide), LOW),
            ((depth, 3 * width), LOW),
        ],
        [slots, place, gains, *saved, *rows, *weights, *mixed],
        [
            pltpu.VMEM((count, wide), LOW),
            pltpu.VMEM((width, depth), LOW),
            pltpu.VMEM((count, depth), LOW),
            pltpu.VMEM((count, width), F32),
            pltpu.VMEM((count, width), LOW),
            pltpu.VMEM((width, wide), LOW),
            pltpu.VMEM((depth, 3 * width), LOW),
            pltpu.SemaphoreType.DMA((layout.parts,)),
            pltpu.SemaphoreType.DMA,
            pltpu.SemaphoreType.DMA((layout.parts,)),
            pltpu.SemaphoreType.DMA((2,)),
            pltpu.SemaphoreType.DMA((6,)),
        ]
        + [pltpu.VMEM(array.shape, array.dtype) for array in saved],
        smem=2,
        any_from=3,
        any_outs=(1, 2),
        after=after,
        cost=(10 * count * width * depth, 4 * count * depth + 8 * depth * width + 30 * count * width),
    )


def mixed_grad_kernel(layout, place, grads, *refs):
    weights_in = refs[: layout.plane_count]
    outs = refs[layout.plane_count : -4]
    weights, staged, sem, out_sem = refs[-4:]
    layout.fill_weights(place[0], weights_in, weights, sem)
    await_copies(weights, sem)
    write_parts(
        layout, outs, staged, out_sem, lambda at: product_nt(grads[at, :], weights[...])
    )
    await_copies(staged, out_sem)


def mixed_grad_parts(layout, place, grads, weights, depth, after):
    count, columns = grads.shape
    return call(
        functools.partial(mixed_grad_kernel, layout),
        "mixed_grad_parts",
        part_shapes(layout, depth),
        [place, grads, *weights],
        [
            pltpu.VMEM((depth, columns), LOW),
            pltpu.VMEM((count, depth), LOW),
            pltpu.SemaphoreType.DMA,
            pltpu.SemaphoreType.DMA,
        ],
        smem=1,
        any_from=2,
        any_outs=(0, 1),
        after=after,
        cost=(2 * count * columns * depth, 2 * count * depth + 4 * depth * columns),
    )


def glu_rows(rows_ref, grads_ref, weights, acts, at, width):
    pre = product(rows_ref[at, :], weights[:, : 2 * width])
    gate_pre, up_pre = pre[:, :width], pre[:, width:]
    grad_middle = product(grads_ref[at, :], weights[:, 2 * width : 3 * width])
    sig_gate = jax.nn.sigmoid(gate_pre)
    silu_gate = gate_pre * sig_gate
    acts[at, :width] = (
        grad_middle * up_pre * (sig_gate * (1.0 + gate_pre * (1.0 - sig_gate)))
    ).astype(LOW)
    acts[at, width : 2 * width] = (grad_middle * silu_gate).astype(LOW)
    acts[at, 2 * width : 3 * width] = (silu_gate * up_pre).astype(LOW)
    if 3 * width < acts.shape[1]:
        acts[at, 3 * width :] = jnp.zeros((at.size, acts.shape[1] - 3 * width), LOW)


def glu_grads(layout, rows_ref, grads_ref, acts, out, staged, sem, width):
    def over_features(step, _):
        columns = pl.ds(pl.multiple_of(step * TILE, TILE), TILE)
        left = product_tn(rows_ref[:, columns], acts[:, : 2 * width])
        right = product_tn(grads_ref[:, columns], acts[:, 2 * width :])
        value = jnp.concatenate([left, right], axis=1).astype(LOW)
        layout.weight_grads(out, staged, sem, step, value)
        return 0

    lax.fori_loop(0, rows_ref.shape[1] // TILE, over_features, 0)


def glu_first_kernel(layout, first_count, place, *refs):
    rows_in, refs = refs[: layout.row_count], refs[layout.row_count :]
    grads_in, refs = refs[: layout.row_count], refs[layout.row_count :]
    weights_in, refs = refs[:first_count], refs[first_count:]
    (
        acts_out,
        weight_grads,
        rows_ref,
        grads_ref,
        weights,
        acts,
        staged,
        row_sems,
        grad_sems,
        weight_sem,
        acts_sem,
        out_sem,
    ) = refs
    width = layout.split
    layout.fill_weights(place[0], weights_in, weights, weight_sem)
    layout.fill_rows(rows_in, rows_ref, row_sems)
    layout.fill_rows(grads_in, grads_ref, grad_sems)
    await_copies(weights, weight_sem)

    def one(step, _):
        at = layout.step(step)
        layout.await_step(rows_ref, row_sems, step)
        layout.await_step(grads_ref, grad_sems, step)
        glu_rows(rows_ref, grads_ref, weights, acts, at, width)
        send(acts.at[at], acts_out.at[at], acts_sem)
        return 0

    lax.fori_loop(0, layout.steps, one, 0)
    glu_grads(layout, rows_ref, grads_ref, acts, weight_grads, staged, out_sem, width)
    await_copies(acts, acts_sem)
    await_copies(staged, out_sem)


def glu_first(layout, place, rows, grads, weights):
    count = layout.parts * layout.slot_rows
    depth, columns = rows[0].shape[1], weights[0].shape[1]
    sems = pltpu.SemaphoreType.DMA
    return call(
        functools.partial(glu_first_kernel, layout, len(weights)),
        "glu_first",
        [((count, columns), LOW), ((depth, columns), LOW)],
        [place, *rows, *grads, *weights],
        [
            pltpu.VMEM((count, depth), LOW),
            pltpu.VMEM((count, depth), LOW),
            pltpu.VMEM((depth, columns), LOW),
            pltpu.VMEM((count, columns), LOW),
            pltpu.VMEM((depth, columns), LOW),
            sems((layout.parts,)),
            sems((layout.parts,)),
            sems,
            sems,
            sems,
        ],
        smem=1,
        any_from=1,
        any_outs=(0, 1),
        cost=(4 * count * depth * columns, 4 * count * depth + 4 * depth * columns),
    )


def glu_second_kernel(layout, first_count, second_count, place, *refs):
    rows_in, refs = refs[: layout.row_count], refs[layout.row_count :]
    grads_in, refs = refs[: layout.row_count], refs[layout.row_count :]
    first_in, refs = refs[:first_count], refs[first_count:]
    second_in, refs = refs[:second_count], refs[second_count:]
    first_acts_in, acts_out = refs[0], refs[1]
    outs = refs[2:-14]
    (
        rows_ref,
        grads_ref,
        first,
        second,
        first_acts,
        acts,
        row_sems,
        grad_sems,
        first_sem,
        second_sem,
        first_acts_sem,
        acts_sem,
        staged,
        out_sem,
    ) = refs[-14:]
    width = layout.rest
    layout.fill_weights(place[0], second_in, second, second_sem)
    layout.fill_rows(rows_in, rows_ref, row_sems)
    layout.fill_rows(grads_in, grads_ref, grad_sems)
    layout.fill_weights(place[0], first_in, first, first_sem)
    send(first_acts_in.at[:, pl.ds(0, first.shape[1])], first_acts, first_acts_sem)
    await_copies(second, second_sem)

    def one(step, _):
        at = layout.step(step)
        layout.await_step(rows_ref, row_sems, step)
        layout.await_step(grads_ref, grad_sems, step)
        glu_rows(rows_ref, grads_ref, second, acts, at, width)
        send(acts.at[at], acts_out.at[at], acts_sem)
        return 0

    lax.fori_loop(0, layout.steps, one, 0)
    await_copies(first, first_sem)
    await_copies(first_acts, first_acts_sem)
    write_parts(
        layout,
        outs,
        staged,
        out_sem,
        lambda at: product_nt(first_acts[at, :], first[...])
        + product_nt(acts[at, : 2 * width], second[:, : 2 * width]),
    )
    await_copies(acts, acts_sem)
    await_copies(staged, out_sem)


def glu_second(layout, place, rows, grads, first, second, first_acts):
    count = layout.parts * layout.slot_rows
    depth, columns = rows[0].shape[1], second[0].shape[1]
    first_columns = 2 * layout.split
    sems = pltpu.SemaphoreType.DMA
    return call(
        functools.partial(glu_second_kernel, layout, len(first), len(second)),
        "glu_second",
        [((count, columns), LOW)] + part_shapes(layout, depth),
        [place, *rows, *grads, *first, *second, first_acts],
        [
            pltpu.VMEM((count, depth), LOW),
            pltpu.VMEM((count, depth), LOW),
            pltpu.VMEM((depth, first_columns), LOW),
            pltpu.VMEM((depth, columns), LOW),
            pltpu.VMEM((count, first_columns), LOW),
            pltpu.VMEM((count, columns), LOW),
            sems((layout.parts,)),
            sems((layout.parts,)),
            sems,
            sems,
            sems,
            sems,
            pltpu.VMEM((count, depth), LOW),
            sems,
        ],
        smem=1,
        any_from=1,
        any_outs=(0, 1, 2),
        cost=(5 * count * depth * columns, 6 * count * depth + 4 * depth * columns),
    )


def glu_third_kernel(layout, place, *refs):
    rows_in, refs = refs[: layout.row_count], refs[layout.row_count :]
    grads_in, refs = refs[: layout.row_count], refs[layout.row_count :]
    acts_in, weight_grads = refs[:2]
    rows_ref, grads_ref, acts, staged, row_sems, grad_sems, acts_sem, out_sem = refs[2:]
    width = layout.rest
    send(acts_in, acts, acts_sem)
    layout.fill_rows(rows_in, rows_ref, row_sems)
    layout.fill_rows(grads_in, grads_ref, grad_sems)
    for slot in range(layout.parts):
        at = pl.ds(slot * layout.slot_rows, layout.slot_rows)
        await_copies(rows_ref.at[at], row_sems.at[slot])
        await_copies(grads_ref.at[at], grad_sems.at[slot])
    await_copies(acts, acts_sem)
    glu_grads(layout, rows_ref, grads_ref, acts, weight_grads, staged, out_sem, width)
    await_copies(staged, out_sem)


def glu_third(layout, place, rows, grads, acts, after):
    count, columns = acts.shape
    depth = rows[0].shape[1]
    sems = pltpu.SemaphoreType.DMA
    return call(
        functools.partial(glu_third_kernel, layout),
        "glu_third",
        [((depth, columns), LOW)],
        [place, *rows, *grads, acts],
        [
            pltpu.VMEM((count, depth), LOW),
            pltpu.VMEM((count, depth), LOW),
            pltpu.VMEM((count, columns), LOW),
            pltpu.VMEM((depth, columns), LOW),
            sems((layout.parts,)),
            sems((layout.parts,)),
            sems,
            sems,
        ],
        smem=1,
        any_from=1,
        any_outs=(0,),
        after=after,
        token=True,
        cost=(2 * count * depth * columns, 4 * count * depth + 2 * depth * columns),
    )


def output_kernel(layout, first_count, second_count, place, *refs):
    first_in, refs = refs[:first_count], refs[first_count:]
    second_in, refs = refs[:second_count], refs[second_count:]
    first_acts_in, second_acts_in = refs[:2]
    outs = refs[2:-6]
    first, second, first_acts, second_acts, staged, sems = refs[-6:]
    for weights_in, weights, acts_in, acts, width, i in (
        (first_in, first, first_acts_in, first_acts, layout.split, 0),
        (second_in, second, second_acts_in, second_acts, layout.rest, 2),
    ):
        lanes = pl.ds(2 * width, weights.shape[1])
        layout.fill_weights(
            place[0], [piece.at[:, lanes] for piece in weights_in], weights, sems.at[i]
        )
        send(acts_in.at[:, lanes], acts, sems.at[i + 1])
    await_copies(first, sems.at[0])
    await_copies(first_acts, sems.at[1])
    await_copies(second, sems.at[2])
    await_copies(second_acts, sems.at[3])
    write_parts(
        layout,
        outs,
        staged,
        sems.at[4],
        lambda at: product_nt(first_acts[at, :], first[...])
        + product_nt(second_acts[at, :], second[...]),
    )
    await_copies(staged, sems.at[4])


def output_parts(layout, place, first, second, first_acts, second_acts, depth, after):
    count = first_acts.shape[0]
    widths = first_acts.shape[1] - 2 * layout.split, second_acts.shape[1] - 2 * layout.rest
    return call(
        functools.partial(output_kernel, layout, len(first), len(second)),
        "output_parts",
        part_shapes(layout, depth),
        [place, *first, *second, first_acts, second_acts],
        [pltpu.VMEM((depth, width), LOW) for width in widths]
        + [pltpu.VMEM((count, width), LOW) for width in widths]
        + [pltpu.VMEM((count, depth), LOW), pltpu.SemaphoreType.DMA((5,))],
        smem=1,
        any_from=1,
        any_outs=(0, 1),
        after=after,
        token=True,
        cost=(2 * count * depth * sum(widths), 2 * count * depth + 2 * depth * sum(widths)),
    )


def summed(parts, at):
    total = parts[0][at, :]
    if len(parts) > 1:
        half = parts[1].shape[0]
        part = parts[1] if at.start < half else parts[2]
        first = at.start % half
        total = total + part[first : first + ROWS, :].astype(F32)
    return total


def row_steps(count):
    return [slice(first, first + ROWS) for first in range(0, count, ROWS)]


def inverse_rms(values):
    return lax.rsqrt(jnp.mean(values * values, axis=1, keepdims=True) + EPSILON)


def norm_kernel(tokens, gains, out):
    for at in row_steps(tokens.shape[0]):
        values = tokens[at, :].astype(F32)
        out[at, :] = (values * inverse_rms(values) * gains[...]).astype(LOW)


def residual_kernel(tokens, gains, *refs):
    parts, (residual_out, ffn_out, inverse_out) = refs[:-3], refs[-3:]
    width = tokens.shape[1]
    for at in row_steps(tokens.shape[0]):
        total = summed(parts, at)
        squares = total[:, width : width + 1] + total[:, width + 1 : width + 2]
        inverse = lax.rsqrt(squares * (1.0 / width) + EPSILON)
        inverse_out[at, :] = inverse
        residual = tokens[at, :].astype(F32) + total[:, :width] * inverse
        residual_out[at, :] = residual
        ffn_out[at, :] = (residual * inverse_rms(residual) * gains[...]).astype(LOW)


def grad_residual_kernel(tokens, cotangent, gains, residual_in, inverse_in, *refs):
    parts, (grad_out, low_out) = refs[:-2], refs[-2:]
    width = tokens.shape[1]
    for at in row_steps(tokens.shape[0]):
        residual = residual_in[at, :]
        inverse = inverse_rms(residual)
        normed = residual * inverse
        grad_normed = summed(parts, at) * gains[...]
        mean = jnp.mean(grad_normed * normed, axis=1, keepdims=True)
        grad = cotangent[at, :].astype(F32) + inverse * (grad_normed - normed * mean)
        grad_out[at, :] = grad
        low = grad.astype(LOW)
        low_out[at, :width] = low
        branch = residual - tokens[at, :].astype(F32)
        mean = jnp.mean(low.astype(F32) * branch, axis=1, keepdims=True)
        low_out[at, width:] = split_lanes(inverse_in[at, :], mean)


def output_rows_kernel(residual, *refs):
    parts, out = refs[:-1], refs[-1]
    for at in row_steps(residual.shape[0]):
        out[at, :] = (residual[at, :] + summed(parts, at)).astype(LOW)


def grad_tokens_kernel(tokens, gains, grad_residual, *refs):
    parts, out = refs[:-1], refs[-1]
    for at in row_steps(tokens.shape[0]):
        values = tokens[at, :].astype(F32)
        inverse = inverse_rms(values)
        normed = values * inverse
        grad_normed = summed(parts, at) * gains[...]
        mean = jnp.mean(grad_normed * normed, axis=1, keepdims=True)
        out[at, :] = (
            grad_residual[at, :] + inverse * (grad_normed - normed * mean)
        ).astype(LOW)


def add_rows(mine, other, wide):
    total = mine.astype(F32) + other.astype(F32)
    low = total.astype(LOW)
    if wide < total.shape[1]:
        number = jnp.sum(total[:, wide:], axis=1, keepdims=True)
        lanes = split_lanes(number)
        low = jnp.concatenate([low[:, :wide], lanes], axis=1)
        total = jnp.concatenate([total[:, :wide], lanes.astype(F32)], axis=1)
    return (total, low)


def core_sum_kernel(rows, wide, mine, other, top_out, end_out, top_keep, end_keep):
    half = rows // 2
    for x in range(2):
        for y in range(2):
            slot = x * 2 + y
            for first in range(0, rows, ROWS):
                at = slice(slot * rows + first, slot * rows + first + ROWS)
                _, low = add_rows(mine[at, :], other[at, :], wide)
                if first < half:
                    if x:
                        top_out[y * half + first : y * half + first + ROWS, :] = low
                    else:
                        top_keep[y * half + first : y * half + first + ROWS, :] = low
                else:
                    to = x * half + first - half
                    if y:
                        end_out[to : to + ROWS, :] = low
                    else:
                        end_keep[to : to + ROWS, :] = low


def chip_sum_kernel(wide, top, end, top_in, end_in, top_out, end_out, keep):
    half = top.shape[0] // 2
    for i, (mine, other, out) in enumerate(((top, top_in, top_out), (end, end_in, end_out))):
        for first in range(0, half, ROWS):
            at = slice(first, first + ROWS)
            to = i * half + first
            keep[to : to + ROWS, :] = add_rows(mine[at, :], other[at, :], wide)[0]
            at = slice(half + first, half + first + ROWS)
            out[first : first + ROWS, :] = add_rows(mine[at, :], other[at, :], wide)[1]


class Links:
    def __init__(self, sizes):
        self.sizes = sizes
        self.pairs = sizes["y"] == sizes["core"] == sizes["x"] == 2
        self.plane = ("x", "y", "core")
        self.owners = ("y", "core", "x")

    def place(self, axis):
        return lax.axis_index(axis)

    def slots(self):
        sizes = self.sizes
        x, y, core = jnp.meshgrid(
            jnp.arange(sizes["x"]), jnp.arange(sizes["y"]), jnp.arange(sizes["core"]), indexing="ij"
        )
        if self.pairs:
            x, y, core = x ^ self.place("x"), y ^ self.place("y"), core ^ self.place("core")
            slot = (core * 2 + x) * 2 + y
        else:
            slot = (x * sizes["y"] + y) * sizes["core"] + core
        return slot.reshape(-1).astype(jnp.int32)

    def swap(self, axis, value):
        return lax.ppermute(value, axis, SWAP)

    def rows(self, value, after=()):
        if not self.pairs:
            return [lax.all_gather(value, self.plane, axis=0, tiled=True)]
        half = value.shape[0] // 2
        by_x, by_y = self.swap("x", value), self.swap("y", value)
        top, end = call(
            halves_kernel, "halves", [((half, value.shape[1]), LOW)] * 2, [by_x, by_y], after=after
        )
        own = [value, by_y, by_x, self.swap("y", top), self.swap("x", end)]
        return own + [self.swap("core", piece) for piece in own]

    def sum_cores(self, parts, after=(), wide=None):
        if not self.pairs:
            return parts
        away, mine = parts
        rows, width = mine.shape[0] // 4, mine.shape[1]
        return call(
            functools.partial(core_sum_kernel, rows, width if wide is None else wide),
            "core_sum",
            [((rows, width), LOW)] * 4,
            [mine, self.swap("core", away)],
            cost=(8 * rows * width, 24 * rows * width),
            after=after,
            token=True,
        )

    def swap_chips(self, parts):
        return [self.swap("x", parts[0]), self.swap("y", parts[1])] if self.pairs else []

    def sum_chips(self, parts, others, after=(), wide=None):
        if not self.pairs:
            return [
                lax.psum_scatter(parts[0], self.plane, scatter_dimension=0, tiled=True).astype(F32)
            ]
        top, end, top_keep, end_keep, _ = parts
        rows, width = top.shape
        top, end, keep = call(
            functools.partial(chip_sum_kernel, width if wide is None else wide),
            "chip_sum",
            [((rows // 2, width), LOW)] * 2 + [((rows, width), F32)],
            [top_keep, end_keep, *others],
            cost=(2 * rows * width, 12 * rows * width),
            after=after,
        )
        return [keep, self.swap("y", top), self.swap("x", end)]

    def sum_planes_small(self, value):
        planes = self.sizes["z"]
        if not (self.pairs and planes & (planes - 1) == 0):
            return lax.psum(value, "z")
        step = 1
        while step < planes:
            value = value + lax.ppermute(value, "z", [(i, i ^ step) for i in range(planes)])
            step *= 2
        return value

    def sum_plane_small(self, value):
        if not self.pairs:
            return lax.psum(value, self.plane)
        for axis in ("x", "y", "core"):
            value = value + self.swap(axis, value)
        return value

    def exchange(self, value):
        return lax.all_to_all(value, self.owners, split_axis=0, concat_axis=0, tiled=True)

    def ring(self, value, gate=lambda pieces: pieces):
        planes = self.sizes["z"]

        def shift(value, by):
            return lax.ppermute(value, "z", [(i, (i + by) % planes) for i in range(planes)])

        pieces = {0: value, 1: shift(value, 1)}
        if planes > 2:
            pieces[planes - 1] = shift(value, -1)
        pieces.update(zip([k for k in pieces if k], gate([pieces[k] for k in pieces if k])))
        for k in range(2, planes - 1):
            pieces[k] = shift(pieces[k - 1], 1)
        return [pieces[k] for k in range(planes)]

    def sum_planes(self, value):
        return lax.psum_scatter(value, "z", scatter_dimension=0, tiled=True)

    def both_x(self, value):
        if self.sizes["x"] == 1:
            return value
        if self.sizes["x"] != 2:
            return lax.all_gather(value, "x", axis=0, tiled=True)
        other = self.swap("x", value)
        return jnp.where(
            self.place("x") == 0,
            jnp.concatenate([value, other], axis=0),
            jnp.concatenate([other, value], axis=0),
        )


def on_device(
    sizes,
    tokens,
    doc_lengths,
    w_in,
    w_forget,
    w_gate_out,
    w_out,
    w_gate,
    w_up,
    w_down,
    g_mix,
    g_out,
    g_ffn,
    floor_logit,
    cotangent,
):
    links = Links(sizes)
    tokens, cotangent = tokens[0], cotangent[0]
    row_count, width = tokens.shape
    block = w_in.shape[0]
    hidden = w_gate.shape[1]
    layout = Layout(sizes, row_count, block, hidden)
    seq, planes, buckets, parts = layout.seq, layout.planes, layout.buckets, layout.parts
    slab = width // parts
    seq_place = links.place("y") * sizes["core"] + links.place("core")
    x_place, z_place = links.place("x"), links.place("z")
    owner = (seq_place * planes + z_place) * buckets + x_place
    place = z_place.astype(jnp.int32).reshape(1)
    wide, low_wide = ((row_count, width), F32), ((row_count, width), LOW)
    column = ((row_count, 1), F32)
    row_cost = (20 * row_count * width, 8 * row_count * width)

    def own_channels(vector):
        return lax.dynamic_index_in_dim(
            lax.dynamic_index_in_dim(
                vector.reshape(-1, seq, planes, buckets, block), seq_place, 1, keepdims=False
            ),
            x_place,
            2,
            keepdims=False,
        ).reshape(-1, slab)

    def to_hidden(first, size, after):
        return call(
            functools.partial(to_hidden_kernel, layout, first, size),
            "to_hidden",
            [((parts, block, -(-3 * size // 128) * 128), LOW)],
            [w_gate, w_up, w_down],
            after=after,
        )[0]

    def gather_weights(weight, ring=True, gate=lambda pieces: pieces):
        weight = weight.reshape(parts * block, -1)
        if layout.pieces and ring:
            return links.ring(weight, gate)
        if layout.pieces:
            return [lax.all_gather(weight, "z", axis=0, tiled=True)]
        full = lax.all_gather(weight, "z", axis=0)
        full = full.reshape(planes, seq, layout.strip, -1)
        return [jnp.swapaxes(full, 0, 1).reshape(width, -1)]

    def gather_channels(weight):
        if layout.pieces:
            return links.ring(weight)
        return [lax.all_gather(weight, "z", axis=0, tiled=True)]

    def scatter_weights(grads):
        if not layout.pieces:
            grads = grads.reshape(seq, planes, layout.strip, -1)
            grads = jnp.swapaxes(grads, 0, 1).reshape(width, -1)
        return links.sum_planes(grads).reshape(parts, block, -1)

    (mixer,) = call(
        functools.partial(to_channels_kernel, layout),
        "to_channels",
        [((parts, block, 3 * slab), LOW)],
        [w_in, w_forget, w_gate_out],
    )
    vectors = jnp.stack([g_mix, g_ffn, g_out, floor_logit]).astype(F32)
    vectors = links.sum_planes_small(
        lax.dynamic_update_slice(jnp.zeros((4, width), F32), vectors, (0, owner * block))
    )
    out_weights = [lax.all_gather(w_out, "z", axis=0, tiled=True)]
    arrived = pin(links.exchange(mixer), [vectors, *out_weights])
    vectors = links.sum_plane_small(vectors)
    gain_mix, gain_ffn = vectors[0:1], vectors[1:2]
    own_vectors = own_channels(vectors[2:])
    gain_out = own_vectors[0:1]
    floors = jax.nn.sigmoid(own_vectors[1:2])
    slots = links.slots()
    ends = links.both_x(jnp.cumsum(doc_lengths, axis=1).astype(jnp.int32))

    (mixed,) = call(
        norm_kernel, "mixed_in", [low_wide], [tokens, gain_mix], cost=row_cost, after=[arrived]
    )
    first = links.exchange(to_hidden(0, layout.split, [mixed]))
    mixed = links.rows(mixed)
    mixer = gather_weights(
        arrived,
        gate=lambda pieces: [pin(pieces[0], [*pieces[1:], first, *mixed]), *pieces[1:]],
    )
    grads_all = links.rows(hold(cotangent, mixer[1:2]))
    first = gather_weights(pin(first, mixer[1:2]), False)
    second = links.exchange(to_hidden(layout.split, layout.rest, mixer[1:2]))
    late = [second]
    second = gather_weights(second, False)
    forget, floor_term, slope_forget, slope_input, gate_pre, states, scaled = mixer_forward(
        layout, slots, ends, place, floors, gain_out, mixed, mixer, []
    )
    branch = branch_parts(layout, place, scaled, states, out_weights, late + grads_all[3:5])
    branch = links.sum_cores(branch, wide=width)
    branch = links.sum_chips(branch, links.swap_chips(branch), wide=width)
    residual, ffn, inverse_h = call(
        residual_kernel,
        "residual",
        [wide, low_wide, column],
        [tokens, gain_ffn, *branch],
        cost=row_cost,
    )

    ffn = links.rows(ffn)
    first_acts, first_grads = glu_first(layout, place, ffn, grads_all, first)
    first_grads = scatter_weights(first_grads)
    second_acts, *ffn_parts = glu_second(
        layout, place, ffn, grads_all, first, second, first_acts
    )
    ffn_parts = links.sum_cores(ffn_parts)
    others = links.swap_chips(ffn_parts)
    second_grads, token = glu_third(
        layout, place, ffn, grads_all, second_acts, ffn_parts[-1:]
    )
    second_grads = scatter_weights(pin(second_grads, others))
    grad_ffn = links.sum_chips(ffn_parts, others, [token])
    grad_residual, grad_low, token = call(
        grad_residual_kernel,
        "grad_residual",
        [wide, ((row_count, width + 128), LOW)],
        [tokens, cotangent, gain_ffn, residual, inverse_h, *grad_ffn],
        cost=row_cost,
        token=True,
    )

    *out_parts, token = output_parts(
        layout, place, first, second, first_acts, second_acts, width, [token]
    )
    grads_low = links.rows(grad_low, [token])
    out_parts = [pin(out_parts[0], grads_low[1:3]), *out_parts[1:]]
    output = links.sum_cores(out_parts, grads_low[3:5])
    saved = [gate_pre, states, forget, floor_term, slope_forget, slope_input]
    mixer_grads, out_grads, mixer_weight_grads = mixer_backward(
        layout, slots, place, gain_out, saved, grads_low, out_weights, mixed, output[-1:]
    )
    mixer_weight_grads = scatter_weights(mixer_weight_grads)
    out_grads = links.sum_planes(out_grads)
    mixed_parts = links.sum_cores(
        mixed_grad_parts(layout, place, mixer_grads, mixer, width, [])
    )
    first_grads = links.exchange(hold(first_grads, mixed_parts[-1:]))
    output = links.sum_chips(output, links.swap_chips(output))
    (output,) = call(
        output_rows_kernel, "output_rows", [low_wide], [residual, *output], cost=row_cost
    )
    grad_mixed = links.sum_chips(mixed_parts, links.swap_chips(mixed_parts))
    grad_tokens, token = call(
        grad_tokens_kernel,
        "grad_tokens",
        [low_wide],
        [tokens, gain_mix, grad_residual, *grad_mixed],
        cost=row_cost,
        token=True,
        after=[output, first_grads],
    )
    second_grads = links.exchange(hold(second_grads, [token]))
    mixer_weight_grads = links.exchange(pin(mixer_weight_grads, [second_grads]))

    def as_column(vector):
        return vector.astype(F32).reshape(block, 1)

    square, long, single = ((block, width), F32), ((block, hidden), F32), ((block, 1), F32)
    gate_w, up_w, down_w, grad_g_ffn = call(
        functools.partial(from_hidden_kernel, layout),
        "from_hidden",
        [long] * 3 + [single],
        [first_grads, second_grads, as_column(g_ffn), w_gate, w_up],
    )
    out_w, grad_g_out, grad_floor = call(
        channel_gain_kernel,
        "from_out",
        [square, single, single],
        [out_grads, w_out, as_column(g_out), as_column(floor_logit)],
    )
    in_w, forget_w, gate_out_w, grad_g_mix = call(
        functools.partial(from_channels_kernel, layout),
        "from_channels",
        [square] * 3 + [single],
        [mixer_weight_grads, as_column(g_mix), w_in, w_forget, w_gate_out],
    )
    return (
        output[None],
        grad_tokens[None],
        in_w,
        forget_w,
        gate_out_w,
        out_w,
        gate_w,
        up_w,
        down_w,
        grad_g_mix.reshape(block),
        grad_g_out.reshape(block),
        grad_g_ffn.reshape(block),
        grad_floor.reshape(block),
    )


def solution(mesh):
    seq, dp = mesh.shape["seq"], mesh.shape["dp"]
    core = 2 if seq % 2 == 0 else 1
    x = max(1, TENSOR_PARTS // seq)
    if dp % x:
        x = 1
    sizes = {"y": seq // core, "core": core, "z": dp // x, "x": x}
    split = Mesh(mesh.devices.reshape(tuple(sizes.values())), tuple(sizes))
    rows = P(("z", "x"), ("y", "core"), None)
    lengths = P(("z", "x"), None)
    matrix = P(("y", "core", "z", "x"), None)
    vector = P(("y", "core", "z", "x"))
    return jax.shard_map(
        functools.partial(on_device, sizes),
        mesh=split,
        in_specs=(rows, lengths) + (matrix,) * 7 + (vector,) * 4 + (rows,),
        out_specs=(rows, rows) + (matrix,) * 7 + (vector,) * 4,
        check_vma=False,
    )
```

```python
import functools
import math

import jax
import jax.numpy as jnp
from jax import lax
from jax.experimental import pallas as pl
from jax.experimental.pallas import tpu as pltpu
from jax.sharding import Mesh
from jax.sharding import PartitionSpec as P

EPSILON = 1e-06
F32 = jnp.float32
LOW = jnp.bfloat16
TENSOR_PARTS = 8
SWAP = [(0, 1), (1, 0)]
ROWS = 16
TILE = 512
SLOTS = 2
COST = 1
VMEM_BYTES = 58 * 1024 * 1024
SPARE_BYTES = 12 * 1024 * 1024
VMEM_SPEC = pl.BlockSpec(memory_space=pltpu.VMEM)
TOKEN = ((8, 128), F32)
SMEM_SPEC = pl.BlockSpec(memory_space=pltpu.SMEM)
ANY_SPEC = pl.BlockSpec(memory_space=pl.ANY)


def product(left_op, right_op):
    return jnp.dot(left_op, right_op, preferred_element_type=F32)


def product_nt(left_op, right_op):
    return lax.dot_general(
        left_op, right_op, (((1,), (1,)), ((), ())), preferred_element_type=F32
    )


def product_tn(left_op, right_op):
    return lax.dot_general(
        left_op, right_op, (((0,), (0,)), ((), ())), preferred_element_type=F32
    )


def call(
    kernel,
    name,
    outs,
    operands,
    scratch=(),
    smem=0,
    any_from=None,
    any_outs=(),
    cost=(0, 0),
    after=(),
    token=False,
):
    any_from = len(operands) if any_from is None else any_from
    if after:
        inner, count, extra = kernel, len(operands), len(after)

        def kernel(*refs):
            inner(*refs[:count], *refs[count + extra :])

        operands = list(operands) + list(after)
        any_from = min(any_from, count)
    if token:
        plain, mark = kernel, len(operands) + len(outs)

        def kernel(*refs):
            refs[mark][...] = jnp.zeros(TOKEN[0], F32)
            plain(*refs[:mark], *refs[mark + 1 :])

        any_outs = [i for i in any_outs if i < len(outs)]
        outs = list(outs) + [TOKEN]
    held = list(operands[smem:any_from]) + [
        jax.ShapeDtypeStruct(*out) for i, out in enumerate(outs) if i not in any_outs
    ]
    held = sum(math.prod(array.shape) * array.dtype.itemsize for array in held)
    specs = [
        SMEM_SPEC if i < smem else (ANY_SPEC if i >= any_from else VMEM_SPEC)
        for i in range(len(operands))
    ]
    return pl.pallas_call(
        kernel,
        out_shape=tuple(jax.ShapeDtypeStruct(*out) for out in outs),
        in_specs=specs,
        out_specs=tuple(ANY_SPEC if i in any_outs else VMEM_SPEC for i in range(len(outs))),
        scratch_shapes=list(scratch),
        compiler_params=pltpu.CompilerParams(
            vmem_limit_bytes=VMEM_BYTES if scratch else held + SPARE_BYTES
        ),
        cost_estimate=pl.CostEstimate(
            flops=int(cost[0] * COST), bytes_accessed=int(cost[1] * COST), transcendentals=0
        ),
        name=name,
    )(*operands)


def await_copies(view, sem):
    pltpu.make_async_copy(view, view, sem).wait()


def send(source, target, sem):
    pltpu.make_async_copy(source, target, sem).start()


class Layout:
    def __init__(self, sizes, slot_rows, block, hidden):
        self.seq = sizes["y"] * sizes["core"]
        self.planes = sizes["z"]
        self.buckets = sizes["x"]
        self.parts = self.seq * self.buckets
        self.slot_rows = slot_rows
        self.block = block
        share = hidden // self.parts
        self.split = -(-share // 256) * 128
        self.rest = share - self.split
        self.pieces = sizes["y"] == sizes["core"] == sizes["x"] == 2
        self.strip = self.buckets * block
        half = slot_rows // 2
        self.row_pieces = (
            [(c + s, r) for c in (0, 4) for s, r in ((0, 0), (1, 0), (2, 0), (3, 0), (3, half))]
            if self.pieces
            else [(0, 0)]
        )
        self.row_count = len(self.row_pieces)
        self.plane_count = self.planes if self.pieces else 1
        self.step_rows = SLOTS * slot_rows
        self.steps = self.parts // SLOTS

    def step(self, index):
        return pl.ds(pl.multiple_of(index * self.step_rows, self.step_rows), self.step_rows)

    def await_step(self, target, sems, index):
        for i in range(SLOTS):
            slot = index * SLOTS + i
            first = pl.multiple_of(slot * self.slot_rows, self.slot_rows)
            await_copies(target.at[pl.ds(first, self.slot_rows)], sems.at[slot])

    def fill_rows(self, pieces, target, sems):
        if not self.pieces:
            for slot in range(self.parts):
                at = pl.ds(slot * self.slot_rows, self.slot_rows)
                send(pieces[0].at[at], target.at[at], sems.at[slot])
            return
        for piece, (slot, first) in zip(pieces, self.row_pieces):
            at = pl.ds(slot * self.slot_rows + first, piece.shape[0])
            send(piece, target.at[at], sems.at[slot])

    def fill_weights(self, place, pieces, target, sem, columns=None):
        columns = target.shape[1] if columns is None else columns
        lanes = pl.ds(0, columns)
        if not self.pieces:
            send(pieces[0].at[:, lanes], target, sem)
            return
        if len(pieces) == 1:
            for plane in range(self.planes):
                for s in range(self.seq):
                    send(
                        pieces[0].at[pl.ds((plane * self.seq + s) * self.strip, self.strip), lanes],
                        target.at[pl.ds((s * self.planes + plane) * self.strip, self.strip)],
                        sem,
                    )
            return
        for step, piece in enumerate(pieces):
            plane = lax.rem(place - step + self.planes, self.planes)
            for s in range(self.seq):
                first = pl.multiple_of((s * self.planes + plane) * self.strip, self.strip)
                send(
                    piece.at[pl.ds(s * self.strip, self.strip), lanes],
                    target.at[pl.ds(first, self.strip)],
                    sem,
                )

    def fill_channels(self, place, pieces, target, sem):
        if len(pieces) == 1:
            send(pieces[0], target, sem)
            return
        for step, piece in enumerate(pieces):
            plane = lax.rem(place - step + self.planes, self.planes)
            first = pl.multiple_of(plane * self.block, self.block)
            send(piece, target.at[pl.ds(first, self.block)], sem)

    def strip_row(self, index):
        if not self.pieces:
            return index * self.strip
        return pl.multiple_of(
            ((index % self.planes) * self.seq + index // self.planes) * self.strip, self.strip
        )

    def weight_grads(self, out, staged, sem, step, value):
        if not self.pieces:
            rows = pl.ds(pl.multiple_of(step * TILE, TILE), TILE)
            staged[rows, :] = value
            send(staged.at[rows], out.at[rows], sem)
            return
        per = TILE // self.strip
        for i in range(per):
            rows = pl.ds(self.strip_row(step * per + i), self.strip)
            staged[rows, :] = value[i * self.strip : (i + 1) * self.strip]
            send(staged.at[rows], out.at[rows], sem)


def row_sums(values):
    lanes = values[:, :128]
    for first in range(128, values.shape[1], 128):
        lanes = lanes + values[:, first : first + 128]
    ones = jnp.ones((8, 128), LOW)
    total = jnp.zeros((8, values.shape[0]), F32)
    for _ in range(3):
        high = lanes.astype(LOW)
        total = total + product_nt(ones, high)
        lanes = lanes - high.astype(F32)
    return total[0:1]


def to_channels_kernel(layout, *refs):
    *weights, out = refs
    block, width = layout.block, layout.block * layout.planes
    for i, weight in enumerate(weights):
        for s in range(layout.seq):
            for z in range(layout.planes):
                for x in range(layout.buckets):
                    first = ((s * layout.planes + z) * layout.buckets + x) * block
                    to = i * width + z * block
                    out[s * layout.buckets + x, :, to : to + block] = weight[
                        :, first : first + block
                    ]


def from_channels_kernel(layout, grads, gains, *refs):
    count = (len(refs) - 1) // 2
    weights, outs, gain_out = refs[:count], refs[count:-1], refs[-1]
    block, width = layout.block, layout.block * layout.planes
    total = jnp.zeros((1, block), F32)
    for i, (weight, out) in enumerate(zip(weights, outs)):
        for s in range(layout.seq):
            for z in range(layout.planes):
                for x in range(layout.buckets):
                    first = ((s * layout.planes + z) * layout.buckets + x) * block
                    at = i * width + z * block
                    out[:, first : first + block] = grads[
                        s * layout.buckets + x, :, at : at + block
                    ].astype(F32)
        total = total + row_sums(out[...] * weight[...].astype(F32))
    gain_out[...] = total / gains[...]


def to_hidden_kernel(layout, first, size, *refs):
    *weights, out = refs
    share = weights[0].shape[1] // layout.parts
    for i, weight in enumerate(weights):
        for part in range(layout.parts):
            at = part * share + first
            out[part, :, i * size : (i + 1) * size] = weight[:, at : at + size]
    used = len(weights) * size
    if used < out.shape[2]:
        out[:, :, used:] = jnp.zeros((layout.parts, layout.block, out.shape[2] - used), LOW)


def from_hidden_kernel(layout, first, second, gains, *refs):
    *weights, gate_out, up_out, down_out, gain_out = refs
    split, rest = layout.split, layout.rest
    share = split + rest
    total = jnp.zeros((1, layout.block), F32)
    for i, out in enumerate((gate_out, up_out, down_out)):
        for part in range(layout.parts):
            at = part * share
            out[:, at : at + split] = first[part, :, i * split : (i + 1) * split].astype(F32)
            out[:, at + split : at + share] = second[part, :, i * rest : (i + 1) * rest].astype(F32)
        if i < len(weights):
            total = total + row_sums(out[...] * weights[i][...].astype(F32))
    gain_out[...] = total / gains[...]


def channel_gain_kernel(grads, weight, gains, floors, out, gain_out, floor_out):
    width = weight.shape[1]
    out[...] = grads[:, :width].astype(F32)
    gain_out[...] = row_sums(out[...] * weight[...].astype(F32)) / gains[...]
    floor = jax.nn.sigmoid(floors[...])
    lane = lax.broadcasted_iota(jnp.int32, (grads.shape[0], 128), 1)
    total = row_sums(jnp.where(lane == 0, grads[:, width:].astype(F32), 0.0))
    floor_out[...] = total * floor * (1.0 - floor)


def hold_kernel(value, out):
    out[...] = value[...]


def hold(value, after):
    return call(hold_kernel, "hold", [(value.shape, value.dtype)], [value], after=after)[0]


def pin_kernel(value, *refs):
    del value, refs


def pin(value, after):
    return pl.pallas_call(
        pin_kernel,
        out_shape=jax.ShapeDtypeStruct(value.shape, value.dtype),
        in_specs=[ANY_SPEC] * (1 + len(after)),
        out_specs=ANY_SPEC,
        input_output_aliases={0: 0},
        name="pin",
    )(value, *after)


def halves_kernel(by_x, by_y, top, end):
    half = top.shape[0]
    top[...] = by_x[:half, :]
    end[...] = by_y[half:, :]


def row_marks(ends, bucket, first, shape):
    rows = first + lax.broadcasted_iota(jnp.int32, shape, 0)
    docs = ends.shape[1]
    hit = rows == 0
    for doc in range(docs - 1):
        hit = jnp.logical_or(hit, rows == ends[bucket, doc])
    keep = jnp.where(hit, 0.0, 1.0)
    live = jnp.where(rows < ends[bucket, docs - 1], 1.0, 0.0)
    return (keep, live)


def prefix(decay, term, forward):
    rows = lax.broadcasted_iota(jnp.int32, decay.shape, 0)
    for step in (1, 2, 4):
        shift = step if forward else 8 - step
        inside = rows >= step if forward else rows < 8 - step
        moved_term = jnp.where(inside, pltpu.roll(term, shift, 0), 0.0)
        moved_decay = jnp.where(inside, pltpu.roll(decay, shift, 0), 1.0)
        term = term + decay * moved_term
        decay = decay * moved_decay
    return (decay, term)


def mixer_forward_kernel(
    layout,
    slots,
    ends,
    place,
    floors,
    gains,
    *refs,
):
    rows_in = refs[: layout.row_count]
    weights_in = refs[layout.row_count : layout.row_count + layout.plane_count]
    outs, refs = refs[layout.row_count + layout.plane_count :][:7], refs[-13:]
    rows_ref, weights, pre, row_sems, weight_sem, out_sems, *kept = refs
    (
        forget_out,
        floor_out,
        slope_forget_out,
        slope_input_out,
        gate_out,
        states_out,
        scaled_out,
    ) = kept
    width = floors.shape[1]
    seg_rows = layout.slot_rows
    buckets, segments = layout.buckets, layout.seq
    layout.fill_weights(place[0], weights_in, weights, weight_sem)
    layout.fill_rows(rows_in, rows_ref, row_sems)
    await_copies(weights, weight_sem)

    def multiply(step, _):
        at = layout.step(step)
        layout.await_step(rows_ref, row_sems, step)
        pre[at, :] = product(rows_ref[at, :], weights[...])
        return 0

    lax.fori_loop(0, layout.steps, multiply, 0)
    floor = floors[...]
    gain = gains[...]
    first_row = lax.broadcasted_iota(jnp.int32, (8, width), 0) == 0

    def one(bucket, segment, block, carry):
        base = pl.multiple_of(slots[bucket * segments + segment] * seg_rows + block * ROWS, ROWS)
        at = pl.ds(base, ROWS)
        keep, live = row_marks(ends, bucket, segment * seg_rows + block * ROWS, (ROWS, width))
        input_pre = pre[at, :width].astype(LOW).astype(F32)
        forget_pre = pre[at, width : 2 * width].astype(LOW).astype(F32)
        gate_pre = pre[at, 2 * width :]
        gate_out[at, :] = gate_pre
        sig_forget = jax.nn.sigmoid(forget_pre)
        forget = (floor + (1.0 - floor) * sig_forget) * keep
        sig_input = jax.nn.sigmoid(input_pre)
        drive = input_pre * sig_input * live
        term = (1.0 - forget) * drive
        hidden, previous = [], []
        for low in range(0, ROWS, 8):
            decay_part, term_part = prefix(forget[low : low + 8], term[low : low + 8], True)
            here = term_part + decay_part * carry
            previous.append(jnp.where(first_row, carry, pltpu.roll(here, 1, 0)))
            hidden.append(here)
            carry = here[7:8]
        hidden = jnp.concatenate(hidden, axis=0)
        previous = jnp.concatenate(previous, axis=0)
        forget_out[at, :] = forget
        floor_term = (previous - drive) * keep * (1.0 - sig_forget)
        floor_out[at, :] = floor_term
        slope_forget_out[at, :] = floor_term * (1.0 - floor) * sig_forget
        slope_input_out[at, :] = (
            (1.0 - forget) * live * (sig_input * (1.0 + input_pre * (1.0 - sig_input)))
        )
        states = hidden.astype(LOW)
        states_out[at, :] = states
        scaled_out[at, :] = (
            states.astype(F32) * gain * (gate_pre * jax.nn.sigmoid(gate_pre))
        ).astype(LOW)
        return carry

    def over_segments(segment, carries):
        def over_blocks(block, carries):
            return tuple(one(b, segment, block, carries[b]) for b in range(buckets))

        carries = lax.fori_loop(0, seg_rows // ROWS, over_blocks, carries)
        for b in range(buckets):
            first = pl.multiple_of(slots[b * segments + segment] * seg_rows, seg_rows)
            at = pl.ds(first, seg_rows)
            for i, (ref, out) in enumerate(zip(kept, outs)):
                send(ref.at[at], out.at[at], out_sems.at[i])
        return carries

    lax.fori_loop(
        0, segments, over_segments, tuple(jnp.zeros((1, width), F32) for _ in range(buckets))
    )
    for i, ref in enumerate(kept):
        await_copies(ref, out_sems.at[i])


def mixer_forward(layout, slots, ends, place, floors, gains, rows, weights, after):
    count = layout.parts * layout.slot_rows
    width = floors.shape[1]
    depth = rows[0].shape[1]
    wide = (count, width)
    return call(
        functools.partial(mixer_forward_kernel, layout),
        "mixer_forward",
        [(wide, F32)] * 5 + [(wide, LOW)] * 2,
        [slots, ends, place, floors, gains, *rows, *weights],
        [
            pltpu.VMEM((count, depth), LOW),
            pltpu.VMEM((depth, 3 * width), LOW),
            pltpu.VMEM((count, 3 * width), F32),
            pltpu.SemaphoreType.DMA((layout.parts,)),
            pltpu.SemaphoreType.DMA,
            pltpu.SemaphoreType.DMA((7,)),
        ]
        + [pltpu.VMEM(wide, F32)] * 5
        + [pltpu.VMEM(wide, LOW)] * 2,
        smem=3,
        any_from=5,
        any_outs=tuple(range(7)),
        after=after,
        cost=(6 * count * width * depth, 2 * count * depth + 6 * depth * width + 24 * count * width),
    )


def split_lanes(*columns):
    shape = (columns[0].shape[0], 128)
    lane = lax.broadcasted_iota(jnp.int32, shape, 1)
    lanes = jnp.zeros(shape, F32)
    for i, column in enumerate(columns):
        high = column.astype(LOW).astype(F32)
        lanes = jnp.where(lane == 2 * i, high, lanes)
        lanes = jnp.where(lane == 2 * i + 1, column - high, lanes)
    return lanes.astype(LOW)


def branch_kernel(layout, place, scaled, states, *refs):
    weights_in = refs[:1]
    outs = refs[1:-4]
    weights, staged, sem, out_sem = refs[-4:]
    layout.fill_channels(place[0], weights_in, weights, sem)
    await_copies(weights, sem)

    def rows_of(at):
        values = states[at, :].astype(F32)
        squares = jnp.sum(values * values, axis=1, keepdims=True)
        parts = product(scaled[at, :], weights[...]).astype(LOW)
        return jnp.concatenate([parts, split_lanes(squares)], axis=1)

    write_parts(layout, outs, staged, out_sem, rows_of)
    await_copies(staged, out_sem)


def write_parts(layout, outs, staged, sem, rows_of):
    per = layout.steps // len(outs)
    for i, out in enumerate(outs):
        start = (len(outs) - 1 - i) * per

        def one(step, _):
            at = layout.step(start + step)
            staged[at, :] = rows_of(at).astype(LOW)
            send(staged.at[at], out.at[layout.step(step)], sem)
            return 0

        lax.fori_loop(0, per, one, 0)


def part_shapes(layout, width):
    count = layout.parts * layout.slot_rows
    if layout.pieces:
        return [((count // 2, width), LOW)] * 2
    return [((count, width), LOW)]


def branch_parts(layout, place, scaled, states, weights, after):
    count, channels = scaled.shape
    width = weights[0].shape[1]
    return call(
        functools.partial(branch_kernel, layout),
        "branch_parts",
        part_shapes(layout, width + 128),
        [place, scaled, states, *weights],
        [
            pltpu.VMEM((channels, width), LOW),
            pltpu.VMEM((count, width + 128), LOW),
            pltpu.SemaphoreType.DMA,
            pltpu.SemaphoreType.DMA,
        ],
        smem=1,
        any_from=3,
        any_outs=(0, 1),
        after=after,
        cost=(2 * count * channels * width, 2 * count * width + 2 * channels * width),
    )


def mixer_backward_kernel(
    layout,
    slots,
    place,
    gains,
    *refs,
):
    saved, refs = refs[:6], refs[6:]
    rows_in = refs[: layout.row_count]
    refs = refs[layout.row_count :]
    weights_in, refs = refs[:1], refs[1:]
    mixed_in, refs = refs[: layout.row_count], refs[layout.row_count :]
    (
        grads_out,
        out_grads,
        mixer_grads,
        rows_ref,
        weights,
        mixed,
        grad_branch,
        branch,
        staged_out,
        staged,
        row_sems,
        weight_sem,
        mixed_sems,
        out_sems,
        saved_sems,
        *kept,
    ) = refs
    gate_in, states_in, forget_in, floor_in, slope_forget_in, slope_input_in = kept
    width = gains.shape[1]
    depth = weights.shape[1]
    seg_rows = layout.slot_rows
    buckets, segments = layout.buckets, layout.seq
    layout.fill_channels(place[0], weights_in, weights, weight_sem)
    layout.fill_rows(rows_in, rows_ref, row_sems)
    for i, (source, target) in enumerate(zip(saved, kept)):
        send(source, target, saved_sems.at[i])
    layout.fill_rows(mixed_in, mixed, mixed_sems)
    await_copies(weights, weight_sem)

    def multiply(step, _):
        at = layout.step(step)
        layout.await_step(rows_ref, row_sems, step)
        grad_branch[at, :] = product_nt(rows_ref[at, :depth], weights[...])
        return 0

    lax.fori_loop(0, layout.steps, multiply, 0)
    for i, target in enumerate(kept):
        await_copies(target, saved_sems.at[i])
    gain = gains[...]
    last_row = lax.broadcasted_iota(jnp.int32, (8, width), 0) == 7

    def one(bucket, segment, block, carry, floor_sum):
        base = pl.multiple_of(slots[bucket * segments + segment] * seg_rows + block * ROWS, ROWS)
        at = pl.ds(base, ROWS)
        grad_in = grad_branch[at, :]
        gate_pre = gate_in[at, :]
        factors = rows_ref[at, depth : depth + 4].astype(F32)
        inverse = factors[:, 0:1] + factors[:, 1:2]
        mean = factors[:, 2:3] + factors[:, 3:4]
        normed = states_in[at, :].astype(F32) * inverse
        sig_gate = jax.nn.sigmoid(gate_pre)
        silu_gate = gate_pre * sig_gate
        scaled = normed * gain
        branch[at, :] = (scaled * silu_gate).astype(LOW)
        grads_out[at, 2 * width :] = (
            grad_in * scaled * (sig_gate * (1.0 + gate_pre * (1.0 - sig_gate)))
        ).astype(LOW)
        grad_scaled = grad_in * silu_gate
        grad_hidden = (inverse * (grad_scaled * gain - normed * mean)).astype(LOW).astype(F32)
        forget = forget_in[at, :]
        term = forget * grad_hidden
        later = []
        for low in reversed(range(0, ROWS, 8)):
            decay_part, term_part = prefix(forget[low : low + 8], term[low : low + 8], False)
            here = term_part + decay_part * carry
            later.insert(0, jnp.where(last_row, carry, pltpu.roll(here, 7, 0)))
            carry = here[0:1]
        grad_total = grad_hidden + jnp.concatenate(later, axis=0)
        grads_out[at, :width] = (grad_total * slope_input_in[at, :]).astype(LOW)
        grads_out[at, width : 2 * width] = (grad_total * slope_forget_in[at, :]).astype(LOW)
        floor_sum = floor_sum + grad_total * floor_in[at, :]
        return (carry, floor_sum)

    def over_segments(step, state):
        segment = segments - 1 - step

        def over_blocks(block_step, state):
            block = seg_rows // ROWS - 1 - block_step
            carries, floor_sum = state
            fresh = []
            for b in range(buckets):
                carry, floor_sum = one(b, segment, block, carries[b], floor_sum)
                fresh.append(carry)
            return (tuple(fresh), floor_sum)

        return lax.fori_loop(0, seg_rows // ROWS, over_blocks, state)

    zeros = jnp.zeros((ROWS, width), F32)
    carries = tuple(jnp.zeros((1, width), F32) for _ in range(buckets))
    _, floor_sum = lax.fori_loop(0, segments, over_segments, (carries, zeros))
    staged_out[:, :depth] = product_tn(branch[...], rows_ref[:, :depth]).astype(LOW)
    ones = jnp.ones((ROWS, 128), LOW)
    high = floor_sum.astype(LOW)
    rest = (floor_sum - high.astype(F32)).astype(LOW)
    staged_out[:, depth:] = (product_tn(high, ones) + product_tn(rest, ones)).astype(LOW)
    send(staged_out, out_grads, out_sems.at[0])
    for slot in range(layout.parts):
        at = pl.ds(slot * seg_rows, seg_rows)
        await_copies(mixed.at[at], mixed_sems.at[slot])

    def over_features(step, _):
        columns = pl.ds(pl.multiple_of(step * TILE, TILE), TILE)
        value = product_tn(mixed[:, columns], grads_out[...]).astype(LOW)
        layout.weight_grads(mixer_grads, staged, out_sems.at[1], step, value)
        return 0

    lax.fori_loop(0, mixed.shape[1] // TILE, over_features, 0)
    await_copies(staged_out, out_sems.at[0])
    await_copies(staged, out_sems.at[1])


def mixer_backward(layout, slots, place, gains, saved, rows, weights, mixed, after):
    count = layout.parts * layout.slot_rows
    width = gains.shape[1]
    depth = mixed[0].shape[1]
    wide = depth + 128
    return call(
        functools.partial(mixer_backward_kernel, layout),
        "mixer_backward",
        [
            ((count, 3 * width), LOW),
            ((width, wide), LOW),
            ((depth, 3 * width), LOW),
        ],
        [slots, place, gains, *saved, *rows, *weights, *mixed],
        [
            pltpu.VMEM((count, wide), LOW),
            pltpu.VMEM((width, depth), LOW),
            pltpu.VMEM((count, depth), LOW),
            pltpu.VMEM((count, width), F32),
            pltpu.VMEM((count, width), LOW),
            pltpu.VMEM((width, wide), LOW),
            pltpu.VMEM((depth, 3 * width), LOW),
            pltpu.SemaphoreType.DMA((layout.parts,)),
            pltpu.SemaphoreType.DMA,
            pltpu.SemaphoreType.DMA((layout.parts,)),
            pltpu.SemaphoreType.DMA((2,)),
            pltpu.SemaphoreType.DMA((6,)),
        ]
        + [pltpu.VMEM(array.shape, array.dtype) for array in saved],
        smem=2,
        any_from=3,
        any_outs=(1, 2),
        after=after,
        cost=(10 * count * width * depth, 4 * count * depth + 8 * depth * width + 30 * count * width),
    )


def mixed_grad_kernel(layout, place, grads, *refs):
    weights_in = refs[: layout.plane_count]
    outs = refs[layout.plane_count : -4]
    weights, staged, sem, out_sem = refs[-4:]
    layout.fill_weights(place[0], weights_in, weights, sem)
    await_copies(weights, sem)
    write_parts(
        layout, outs, staged, out_sem, lambda at: product_nt(grads[at, :], weights[...])
    )
    await_copies(staged, out_sem)


def mixed_grad_parts(layout, place, grads, weights, depth, after):
    count, columns = grads.shape
    return call(
        functools.partial(mixed_grad_kernel, layout),
        "mixed_grad_parts",
        part_shapes(layout, depth),
        [place, grads, *weights],
        [
            pltpu.VMEM((depth, columns), LOW),
            pltpu.VMEM((count, depth), LOW),
            pltpu.SemaphoreType.DMA,
            pltpu.SemaphoreType.DMA,
        ],
        smem=1,
        any_from=2,
        any_outs=(0, 1),
        after=after,
        cost=(2 * count * columns * depth, 2 * count * depth + 4 * depth * columns),
    )


def glu_rows(rows_ref, grads_ref, weights, acts, at, width):
    pre = product(rows_ref[at, :], weights[:, : 2 * width])
    gate_pre, up_pre = pre[:, :width], pre[:, width:]
    grad_middle = product(grads_ref[at, :], weights[:, 2 * width : 3 * width])
    sig_gate = jax.nn.sigmoid(gate_pre)
    silu_gate = gate_pre * sig_gate
    acts[at, :width] = (
        grad_middle * up_pre * (sig_gate * (1.0 + gate_pre * (1.0 - sig_gate)))
    ).astype(LOW)
    acts[at, width : 2 * width] = (grad_middle * silu_gate).astype(LOW)
    acts[at, 2 * width : 3 * width] = (silu_gate * up_pre).astype(LOW)
    if 3 * width < acts.shape[1]:
        acts[at, 3 * width :] = jnp.zeros((at.size, acts.shape[1] - 3 * width), LOW)


def glu_grads(layout, rows_ref, grads_ref, acts, out, staged, sem, width):
    def over_features(step, _):
        columns = pl.ds(pl.multiple_of(step * TILE, TILE), TILE)
        left = product_tn(rows_ref[:, columns], acts[:, : 2 * width])
        right = product_tn(grads_ref[:, columns], acts[:, 2 * width :])
        value = jnp.concatenate([left, right], axis=1).astype(LOW)
        layout.weight_grads(out, staged, sem, step, value)
        return 0

    lax.fori_loop(0, rows_ref.shape[1] // TILE, over_features, 0)


def glu_first_kernel(layout, first_count, place, *refs):
    rows_in, refs = refs[: layout.row_count], refs[layout.row_count :]
    grads_in, refs = refs[: layout.row_count], refs[layout.row_count :]
    weights_in, refs = refs[:first_count], refs[first_count:]
    (
        acts_out,
        weight_grads,
        rows_ref,
        grads_ref,
        weights,
        acts,
        staged,
        row_sems,
        grad_sems,
        weight_sem,
        acts_sem,
        out_sem,
    ) = refs
    width = layout.split
    layout.fill_weights(place[0], weights_in, weights, weight_sem)
    layout.fill_rows(rows_in, rows_ref, row_sems)
    layout.fill_rows(grads_in, grads_ref, grad_sems)
    await_copies(weights, weight_sem)

    def one(step, _):
        at = layout.step(step)
        layout.await_step(rows_ref, row_sems, step)
        layout.await_step(grads_ref, grad_sems, step)
        glu_rows(rows_ref, grads_ref, weights, acts, at, width)
        send(acts.at[at], acts_out.at[at], acts_sem)
        return 0

    lax.fori_loop(0, layout.steps, one, 0)
    glu_grads(layout, rows_ref, grads_ref, acts, weight_grads, staged, out_sem, width)
    await_copies(acts, acts_sem)
    await_copies(staged, out_sem)


def glu_first(layout, place, rows, grads, weights):
    count = layout.parts * layout.slot_rows
    depth, columns = rows[0].shape[1], weights[0].shape[1]
    sems = pltpu.SemaphoreType.DMA
    return call(
        functools.partial(glu_first_kernel, layout, len(weights)),
        "glu_first",
        [((count, columns), LOW), ((depth, columns), LOW)],
        [place, *rows, *grads, *weights],
        [
            pltpu.VMEM((count, depth), LOW),
            pltpu.VMEM((count, depth), LOW),
            pltpu.VMEM((depth, columns), LOW),
            pltpu.VMEM((count, columns), LOW),
            pltpu.VMEM((depth, columns), LOW),
            sems((layout.parts,)),
            sems((layout.parts,)),
            sems,
            sems,
            sems,
        ],
        smem=1,
        any_from=1,
        any_outs=(0, 1),
        cost=(4 * count * depth * columns, 4 * count * depth + 4 * depth * columns),
    )


def glu_second_kernel(layout, first_count, second_count, place, *refs):
    rows_in, refs = refs[: layout.row_count], refs[layout.row_count :]
    grads_in, refs = refs[: layout.row_count], refs[layout.row_count :]
    first_in, refs = refs[:first_count], refs[first_count:]
    second_in, refs = refs[:second_count], refs[second_count:]
    first_acts_in, acts_out = refs[0], refs[1]
    outs = refs[2:-14]
    (
        rows_ref,
        grads_ref,
        first,
        second,
        first_acts,
        acts,
        row_sems,
        grad_sems,
        first_sem,
        second_sem,
        first_acts_sem,
        acts_sem,
        staged,
        out_sem,
    ) = refs[-14:]
    width = layout.rest
    layout.fill_weights(place[0], second_in, second, second_sem)
    layout.fill_rows(rows_in, rows_ref, row_sems)
    layout.fill_rows(grads_in, grads_ref, grad_sems)
    layout.fill_weights(place[0], first_in, first, first_sem)
    send(first_acts_in.at[:, pl.ds(0, first.shape[1])], first_acts, first_acts_sem)
    await_copies(second, second_sem)

    def one(step, _):
        at = layout.step(step)
        layout.await_step(rows_ref, row_sems, step)
        layout.await_step(grads_ref, grad_sems, step)
        glu_rows(rows_ref, grads_ref, second, acts, at, width)
        send(acts.at[at], acts_out.at[at], acts_sem)
        return 0

    lax.fori_loop(0, layout.steps, one, 0)
    await_copies(first, first_sem)
    await_copies(first_acts, first_acts_sem)
    write_parts(
        layout,
        outs,
        staged,
        out_sem,
        lambda at: product_nt(first_acts[at, :], first[...])
        + product_nt(acts[at, : 2 * width], second[:, : 2 * width]),
    )
    await_copies(acts, acts_sem)
    await_copies(staged, out_sem)


def glu_second(layout, place, rows, grads, first, second, first_acts):
    count = layout.parts * layout.slot_rows
    depth, columns = rows[0].shape[1], second[0].shape[1]
    first_columns = 2 * layout.split
    sems = pltpu.SemaphoreType.DMA
    return call(
        functools.partial(glu_second_kernel, layout, len(first), len(second)),
        "glu_second",
        [((count, columns), LOW)] + part_shapes(layout, depth),
        [place, *rows, *grads, *first, *second, first_acts],
        [
            pltpu.VMEM((count, depth), LOW),
            pltpu.VMEM((count, depth), LOW),
            pltpu.VMEM((depth, first_columns), LOW),
            pltpu.VMEM((depth, columns), LOW),
            pltpu.VMEM((count, first_columns), LOW),
            pltpu.VMEM((count, columns), LOW),
            sems((layout.parts,)),
            sems((layout.parts,)),
            sems,
            sems,
            sems,
            sems,
            pltpu.VMEM((count, depth), LOW),
            sems,
        ],
        smem=1,
        any_from=1,
        any_outs=(0, 1, 2),
        cost=(5 * count * depth * columns, 6 * count * depth + 4 * depth * columns),
    )


def glu_third_kernel(layout, place, *refs):
    rows_in, refs = refs[: layout.row_count], refs[layout.row_count :]
    grads_in, refs = refs[: layout.row_count], refs[layout.row_count :]
    acts_in, weight_grads = refs[:2]
    rows_ref, grads_ref, acts, staged, row_sems, grad_sems, acts_sem, out_sem = refs[2:]
    width = layout.rest
    send(acts_in, acts, acts_sem)
    layout.fill_rows(rows_in, rows_ref, row_sems)
    layout.fill_rows(grads_in, grads_ref, grad_sems)
    for slot in range(layout.parts):
        at = pl.ds(slot * layout.slot_rows, layout.slot_rows)
        await_copies(rows_ref.at[at], row_sems.at[slot])
        await_copies(grads_ref.at[at], grad_sems.at[slot])
    await_copies(acts, acts_sem)
    glu_grads(layout, rows_ref, grads_ref, acts, weight_grads, staged, out_sem, width)
    await_copies(staged, out_sem)


def glu_third(layout, place, rows, grads, acts, after):
    count, columns = acts.shape
    depth = rows[0].shape[1]
    sems = pltpu.SemaphoreType.DMA
    return call(
        functools.partial(glu_third_kernel, layout),
        "glu_third",
        [((depth, columns), LOW)],
        [place, *rows, *grads, acts],
        [
            pltpu.VMEM((count, depth), LOW),
            pltpu.VMEM((count, depth), LOW),
            pltpu.VMEM((count, columns), LOW),
            pltpu.VMEM((depth, columns), LOW),
            sems((layout.parts,)),
            sems((layout.parts,)),
            sems,
            sems,
        ],
        smem=1,
        any_from=1,
        any_outs=(0,),
        after=after,
        token=True,
        cost=(2 * count * depth * columns, 4 * count * depth + 2 * depth * columns),
    )


def output_kernel(layout, first_count, second_count, place, *refs):
    first_in, refs = refs[:first_count], refs[first_count:]
    second_in, refs = refs[:second_count], refs[second_count:]
    first_acts_in, second_acts_in = refs[:2]
    outs = refs[2:-6]
    first, second, first_acts, second_acts, staged, sems = refs[-6:]
    for weights_in, weights, acts_in, acts, width, i in (
        (first_in, first, first_acts_in, first_acts, layout.split, 0),
        (second_in, second, second_acts_in, second_acts, layout.rest, 2),
    ):
        lanes = pl.ds(2 * width, weights.shape[1])
        layout.fill_weights(
            place[0], [piece.at[:, lanes] for piece in weights_in], weights, sems.at[i]
        )
        send(acts_in.at[:, lanes], acts, sems.at[i + 1])
    await_copies(first, sems.at[0])
    await_copies(first_acts, sems.at[1])
    await_copies(second, sems.at[2])
    await_copies(second_acts, sems.at[3])
    write_parts(
        layout,
        outs,
        staged,
        sems.at[4],
        lambda at: product_nt(first_acts[at, :], first[...])
        + product_nt(second_acts[at, :], second[...]),
    )
    await_copies(staged, sems.at[4])


def output_parts(layout, place, first, second, first_acts, second_acts, depth, after):
    count = first_acts.shape[0]
    widths = first_acts.shape[1] - 2 * layout.split, second_acts.shape[1] - 2 * layout.rest
    return call(
        functools.partial(output_kernel, layout, len(first), len(second)),
        "output_parts",
        part_shapes(layout, depth),
        [place, *first, *second, first_acts, second_acts],
        [pltpu.VMEM((depth, width), LOW) for width in widths]
        + [pltpu.VMEM((count, width), LOW) for width in widths]
        + [pltpu.VMEM((count, depth), LOW), pltpu.SemaphoreType.DMA((5,))],
        smem=1,
        any_from=1,
        any_outs=(0, 1),
        after=after,
        token=True,
        cost=(2 * count * depth * sum(widths), 2 * count * depth + 2 * depth * sum(widths)),
    )


def summed(parts, at):
    total = parts[0][at, :]
    if len(parts) > 1:
        half = parts[1].shape[0]
        part = parts[1] if at.start < half else parts[2]
        first = at.start % half
        total = total + part[first : first + ROWS, :].astype(F32)
    return total


def row_steps(count):
    return [slice(first, first + ROWS) for first in range(0, count, ROWS)]


def inverse_rms(values):
    return lax.rsqrt(jnp.mean(values * values, axis=1, keepdims=True) + EPSILON)


def norm_kernel(tokens, gains, out):
    for at in row_steps(tokens.shape[0]):
        values = tokens[at, :].astype(F32)
        out[at, :] = (values * inverse_rms(values) * gains[...]).astype(LOW)


def residual_kernel(tokens, gains, *refs):
    parts, (residual_out, ffn_out, inverse_out) = refs[:-3], refs[-3:]
    width = tokens.shape[1]
    for at in row_steps(tokens.shape[0]):
        total = summed(parts, at)
        squares = total[:, width : width + 1] + total[:, width + 1 : width + 2]
        inverse = lax.rsqrt(squares * (1.0 / width) + EPSILON)
        inverse_out[at, :] = inverse
        residual = tokens[at, :].astype(F32) + total[:, :width] * inverse
        residual_out[at, :] = residual
        ffn_out[at, :] = (residual * inverse_rms(residual) * gains[...]).astype(LOW)


def grad_residual_kernel(tokens, cotangent, gains, residual_in, inverse_in, *refs):
    parts, (grad_out, low_out) = refs[:-2], refs[-2:]
    width = tokens.shape[1]
    for at in row_steps(tokens.shape[0]):
        residual = residual_in[at, :]
        inverse = inverse_rms(residual)
        normed = residual * inverse
        grad_normed = summed(parts, at) * gains[...]
        mean = jnp.mean(grad_normed * normed, axis=1, keepdims=True)
        grad = cotangent[at, :].astype(F32) + inverse * (grad_normed - normed * mean)
        grad_out[at, :] = grad
        low = grad.astype(LOW)
        low_out[at, :width] = low
        branch = residual - tokens[at, :].astype(F32)
        mean = jnp.mean(low.astype(F32) * branch, axis=1, keepdims=True)
        low_out[at, width:] = split_lanes(inverse_in[at, :], mean)


def output_rows_kernel(residual, *refs):
    parts, out = refs[:-1], refs[-1]
    for at in row_steps(residual.shape[0]):
        out[at, :] = (residual[at, :] + summed(parts, at)).astype(LOW)


def grad_tokens_kernel(tokens, gains, grad_residual, *refs):
    parts, out = refs[:-1], refs[-1]
    for at in row_steps(tokens.shape[0]):
        values = tokens[at, :].astype(F32)
        inverse = inverse_rms(values)
        normed = values * inverse
        grad_normed = summed(parts, at) * gains[...]
        mean = jnp.mean(grad_normed * normed, axis=1, keepdims=True)
        out[at, :] = (
            grad_residual[at, :] + inverse * (grad_normed - normed * mean)
        ).astype(LOW)


def add_rows(mine, other, wide):
    total = mine.astype(F32) + other.astype(F32)
    low = total.astype(LOW)
    if wide < total.shape[1]:
        number = jnp.sum(total[:, wide:], axis=1, keepdims=True)
        lanes = split_lanes(number)
        low = jnp.concatenate([low[:, :wide], lanes], axis=1)
        total = jnp.concatenate([total[:, :wide], lanes.astype(F32)], axis=1)
    return (total, low)


def core_sum_kernel(rows, wide, mine, other, top_out, end_out, top_keep, end_keep):
    half = rows // 2
    for x in range(2):
        for y in range(2):
            slot = x * 2 + y
            for first in range(0, rows, ROWS):
                at = slice(slot * rows + first, slot * rows + first + ROWS)
                _, low = add_rows(mine[at, :], other[at, :], wide)
                if first < half:
                    if x:
                        top_out[y * half + first : y * half + first + ROWS, :] = low
                    else:
                        top_keep[y * half + first : y * half + first + ROWS, :] = low
                else:
                    to = x * half + first - half
                    if y:
                        end_out[to : to + ROWS, :] = low
                    else:
                        end_keep[to : to + ROWS, :] = low


def chip_sum_kernel(wide, top, end, top_in, end_in, top_out, end_out, keep):
    half = top.shape[0] // 2
    for i, (mine, other, out) in enumerate(((top, top_in, top_out), (end, end_in, end_out))):
        for first in range(0, half, ROWS):
            at = slice(first, first + ROWS)
            to = i * half + first
            keep[to : to + ROWS, :] = add_rows(mine[at, :], other[at, :], wide)[0]
            at = slice(half + first, half + first + ROWS)
            out[first : first + ROWS, :] = add_rows(mine[at, :], other[at, :], wide)[1]


class Links:
    def __init__(self, sizes):
        self.sizes = sizes
        self.pairs = sizes["y"] == sizes["core"] == sizes["x"] == 2
        self.plane = ("x", "y", "core")
        self.owners = ("y", "core", "x")

    def place(self, axis):
        return lax.axis_index(axis)

    def slots(self):
        sizes = self.sizes
        x, y, core = jnp.meshgrid(
            jnp.arange(sizes["x"]), jnp.arange(sizes["y"]), jnp.arange(sizes["core"]), indexing="ij"
        )
        if self.pairs:
            x, y, core = x ^ self.place("x"), y ^ self.place("y"), core ^ self.place("core")
            slot = (core * 2 + x) * 2 + y
        else:
            slot = (x * sizes["y"] + y) * sizes["core"] + core
        return slot.reshape(-1).astype(jnp.int32)

    def swap(self, axis, value):
        return lax.ppermute(value, axis, SWAP)

    def rows(self, value, after=()):
        if not self.pairs:
            return [lax.all_gather(value, self.plane, axis=0, tiled=True)]
        half = value.shape[0] // 2
        by_x, by_y = self.swap("x", value), self.swap("y", value)
        top, end = call(
            halves_kernel, "halves", [((half, value.shape[1]), LOW)] * 2, [by_x, by_y], after=after
        )
        own = [value, by_y, by_x, self.swap("y", top), self.swap("x", end)]
        return own + [self.swap("core", piece) for piece in own]

    def sum_cores(self, parts, after=(), wide=None):
        if not self.pairs:
            return parts
        away, mine = parts
        rows, width = mine.shape[0] // 4, mine.shape[1]
        return call(
            functools.partial(core_sum_kernel, rows, width if wide is None else wide),
            "core_sum",
            [((rows, width), LOW)] * 4,
            [mine, self.swap("core", away)],
            cost=(8 * rows * width, 24 * rows * width),
            after=after,
            token=True,
        )

    def swap_chips(self, parts):
        return [self.swap("x", parts[0]), self.swap("y", parts[1])] if self.pairs else []

    def sum_chips(self, parts, others, after=(), wide=None):
        if not self.pairs:
            return [
                lax.psum_scatter(parts[0], self.plane, scatter_dimension=0, tiled=True).astype(F32)
            ]
        top, end, top_keep, end_keep, _ = parts
        rows, width = top.shape
        top, end, keep = call(
            functools.partial(chip_sum_kernel, width if wide is None else wide),
            "chip_sum",
            [((rows // 2, width), LOW)] * 2 + [((rows, width), F32)],
            [top_keep, end_keep, *others],
            cost=(2 * rows * width, 12 * rows * width),
            after=after,
        )
        return [keep, self.swap("y", top), self.swap("x", end)]

    def sum_planes_small(self, value):
        planes = self.sizes["z"]
        if not (self.pairs and planes & (planes - 1) == 0):
            return lax.psum(value, "z")
        step = 1
        while step < planes:
            value = value + lax.ppermute(value, "z", [(i, i ^ step) for i in range(planes)])
            step *= 2
        return value

    def sum_plane_small(self, value):
        if not self.pairs:
            return lax.psum(value, self.plane)
        for axis in ("x", "y", "core"):
            value = value + self.swap(axis, value)
        return value

    def exchange(self, value):
        return lax.all_to_all(value, self.owners, split_axis=0, concat_axis=0, tiled=True)

    def ring(self, value, gate=lambda pieces: pieces):
        planes = self.sizes["z"]

        def shift(value, by):
            return lax.ppermute(value, "z", [(i, (i + by) % planes) for i in range(planes)])

        pieces = {0: value, 1: shift(value, 1)}
        if planes > 2:
            pieces[planes - 1] = shift(value, -1)
        pieces.update(zip([k for k in pieces if k], gate([pieces[k] for k in pieces if k])))
        for k in range(2, planes - 1):
            pieces[k] = shift(pieces[k - 1], 1)
        return [pieces[k] for k in range(planes)]

    def sum_planes(self, value):
        return lax.psum_scatter(value, "z", scatter_dimension=0, tiled=True)

    def both_x(self, value):
        if self.sizes["x"] == 1:
            return value
        if self.sizes["x"] != 2:
            return lax.all_gather(value, "x", axis=0, tiled=True)
        other = self.swap("x", value)
        return jnp.where(
            self.place("x") == 0,
            jnp.concatenate([value, other], axis=0),
            jnp.concatenate([other, value], axis=0),
        )


def on_device(
    sizes,
    tokens,
    doc_lengths,
    w_in,
    w_forget,
    w_gate_out,
    w_out,
    w_gate,
    w_up,
    w_down,
    g_mix,
    g_out,
    g_ffn,
    floor_logit,
    cotangent,
):
    links = Links(sizes)
    tokens, cotangent = tokens[0], cotangent[0]
    row_count, width = tokens.shape
    block = w_in.shape[0]
    hidden = w_gate.shape[1]
    layout = Layout(sizes, row_count, block, hidden)
    seq, planes, buckets, parts = layout.seq, layout.planes, layout.buckets, layout.parts
    slab = width // parts
    seq_place = links.place("y") * sizes["core"] + links.place("core")
    x_place, z_place = links.place("x"), links.place("z")
    owner = (seq_place * planes + z_place) * buckets + x_place
    place = z_place.astype(jnp.int32).reshape(1)
    wide, low_wide = ((row_count, width), F32), ((row_count, width), LOW)
    column = ((row_count, 1), F32)
    row_cost = (20 * row_count * width, 8 * row_count * width)

    def own_channels(vector):
        return lax.dynamic_index_in_dim(
            lax.dynamic_index_in_dim(
                vector.reshape(-1, seq, planes, buckets, block), seq_place, 1, keepdims=False
            ),
            x_place,
            2,
            keepdims=False,
        ).reshape(-1, slab)

    def to_hidden(first, size, after):
        return call(
            functools.partial(to_hidden_kernel, layout, first, size),
            "to_hidden",
            [((parts, block, -(-3 * size // 128) * 128), LOW)],
            [w_gate, w_up, w_down],
            after=after,
        )[0]

    def gather_weights(weight, ring=True, gate=lambda pieces: pieces):
        weight = weight.reshape(parts * block, -1)
        if layout.pieces and ring:
            return links.ring(weight, gate)
        if layout.pieces:
            return [lax.all_gather(weight, "z", axis=0, tiled=True)]
        full = lax.all_gather(weight, "z", axis=0)
        full = full.reshape(planes, seq, layout.strip, -1)
        return [jnp.swapaxes(full, 0, 1).reshape(width, -1)]

    def gather_channels(weight):
        if layout.pieces:
            return links.ring(weight)
        return [lax.all_gather(weight, "z", axis=0, tiled=True)]

    def scatter_weights(grads):
        if not layout.pieces:
            grads = grads.reshape(seq, planes, layout.strip, -1)
            grads = jnp.swapaxes(grads, 0, 1).reshape(width, -1)
        return links.sum_planes(grads).reshape(parts, block, -1)

    (mixer,) = call(
        functools.partial(to_channels_kernel, layout),
        "to_channels",
        [((parts, block, 3 * slab), LOW)],
        [w_in, w_forget, w_gate_out],
    )
    vectors = jnp.stack([g_mix, g_ffn, g_out, floor_logit]).astype(F32)
    vectors = links.sum_planes_small(
        lax.dynamic_update_slice(jnp.zeros((4, width), F32), vectors, (0, owner * block))
    )
    out_weights = [lax.all_gather(w_out, "z", axis=0, tiled=True)]
    arrived = pin(links.exchange(mixer), [vectors, *out_weights])
    vectors = links.sum_plane_small(vectors)
    gain_mix, gain_ffn = vectors[0:1], vectors[1:2]
    own_vectors = own_channels(vectors[2:])
    gain_out = own_vectors[0:1]
    floors = jax.nn.sigmoid(own_vectors[1:2])
    slots = links.slots()
    ends = links.both_x(jnp.cumsum(doc_lengths, axis=1).astype(jnp.int32))

    (mixed,) = call(
        norm_kernel, "mixed_in", [low_wide], [tokens, gain_mix], cost=row_cost, after=[arrived]
    )
    first = links.exchange(to_hidden(0, layout.split, [mixed]))
    mixed = links.rows(mixed)
    mixer = gather_weights(
        arrived,
        gate=lambda pieces: [pin(pieces[0], [*pieces[1:], first, *mixed]), *pieces[1:]],
    )
    grads_all = links.rows(hold(cotangent, mixer[1:2]))
    first = gather_weights(pin(first, mixer[1:2]), False)
    second = links.exchange(to_hidden(layout.split, layout.rest, mixer[1:2]))
    late = [second]
    second = gather_weights(second, False)
    forget, floor_term, slope_forget, slope_input, gate_pre, states, scaled = mixer_forward(
        layout, slots, ends, place, floors, gain_out, mixed, mixer, []
    )
    branch = branch_parts(layout, place, scaled, states, out_weights, late + grads_all[3:5])
    branch = links.sum_cores(branch, wide=width)
    branch = links.sum_chips(branch, links.swap_chips(branch), wide=width)
    residual, ffn, inverse_h = call(
        residual_kernel,
        "residual",
        [wide, low_wide, column],
        [tokens, gain_ffn, *branch],
        cost=row_cost,
    )

    ffn = links.rows(ffn)
    first_acts, first_grads = glu_first(layout, place, ffn, grads_all, first)
    first_grads = scatter_weights(first_grads)
    second_acts, *ffn_parts = glu_second(
        layout, place, ffn, grads_all, first, second, first_acts
    )
    ffn_parts = links.sum_cores(ffn_parts)
    others = links.swap_chips(ffn_parts)
    second_grads, token = glu_third(
        layout, place, ffn, grads_all, second_acts, ffn_parts[-1:]
    )
    second_grads = scatter_weights(pin(second_grads, others))
    grad_ffn = links.sum_chips(ffn_parts, others, [token])
    grad_residual, grad_low, token = call(
        grad_residual_kernel,
        "grad_residual",
        [wide, ((row_count, width + 128), LOW)],
        [tokens, cotangent, gain_ffn, residual, inverse_h, *grad_ffn],
        cost=row_cost,
        token=True,
    )

    *out_parts, token = output_parts(
        layout, place, first, second, first_acts, second_acts, width, [token]
    )
    grads_low = links.rows(grad_low, [token])
    out_parts = [pin(out_parts[0], grads_low[1:3]), *out_parts[1:]]
    output = links.sum_cores(out_parts, grads_low[3:5])
    saved = [gate_pre, states, forget, floor_term, slope_forget, slope_input]
    mixer_grads, out_grads, mixer_weight_grads = mixer_backward(
        layout, slots, place, gain_out, saved, grads_low, out_weights, mixed, output[-1:]
    )
    output = links.sum_chips(output, links.swap_chips(output))
    mixer_weight_grads = scatter_weights(pin(mixer_weight_grads, output[:1]))
    out_grads = links.sum_planes(out_grads)
    mixed_parts = links.sum_cores(
        mixed_grad_parts(layout, place, mixer_grads, mixer, width, output[:1])
    )
    first_grads = links.exchange(hold(first_grads, output[:1]))
    (output,) = call(
        output_rows_kernel, "output_rows", [low_wide], [residual, *output], cost=row_cost
    )
    grad_mixed = links.sum_chips(mixed_parts, links.swap_chips(mixed_parts))
    second_grads = links.exchange(hold(second_grads, [first_grads]))
    grad_tokens, token = call(
        grad_tokens_kernel,
        "grad_tokens",
        [low_wide],
        [tokens, gain_mix, grad_residual, *grad_mixed],
        cost=row_cost,
        token=True,
        after=[output],
    )
    mixer_weight_grads = links.exchange(pin(mixer_weight_grads, [token, second_grads]))

    def as_row(vector):
        return vector.astype(F32).reshape(1, block)

    square, long, single = ((block, width), F32), ((block, hidden), F32), ((1, block), F32)
    gate_w, up_w, down_w, grad_g_ffn = call(
        functools.partial(from_hidden_kernel, layout),
        "from_hidden",
        [long] * 3 + [single],
        [first_grads, second_grads, as_row(g_ffn), w_gate, w_up],
    )
    in_w, forget_w, gate_out_w, grad_g_mix = call(
        functools.partial(from_channels_kernel, layout),
        "from_channels",
        [square] * 3 + [single],
        [mixer_weight_grads, as_row(g_mix), w_in, w_forget, w_gate_out],
        after=[grad_g_ffn],
    )
    out_w, grad_g_out, grad_floor = call(
        channel_gain_kernel,
        "from_out",
        [square, single, single],
        [out_grads, w_out, as_row(g_out), as_row(floor_logit)],
        after=[grad_g_mix],
    )
    return (
        output[None],
        grad_tokens[None],
        in_w,
        forget_w,
        gate_out_w,
        out_w,
        gate_w,
        up_w,
        down_w,
        grad_g_mix.reshape(block),
        grad_g_out.reshape(block),
        grad_g_ffn.reshape(block),
        grad_floor.reshape(block),
    )


def solution(mesh):
    seq, dp = mesh.shape["seq"], mesh.shape["dp"]
    core = 2 if seq % 2 == 0 else 1
    x = max(1, TENSOR_PARTS // seq)
    if dp % x:
        x = 1
    sizes = {"y": seq // core, "core": core, "z": dp // x, "x": x}
    split = Mesh(mesh.devices.reshape(tuple(sizes.values())), tuple(sizes))
    rows = P(("z", "x"), ("y", "core"), None)
    lengths = P(("z", "x"), None)
    matrix = P(("y", "core", "z", "x"), None)
    vector = P(("y", "core", "z", "x"))
    return jax.shard_map(
        functools.partial(on_device, sizes),
        mesh=split,
        in_specs=(rows, lengths) + (matrix,) * 7 + (vector,) * 4 + (rows,),
        out_specs=(rows, rows) + (matrix,) * 7 + (vector,) * 4,
        check_vma=False,
    )
```
